128 devices in a mesh: fsdp: 16 (over y, x), tp: 8 (over z, core).
Axes of the slice: x: 4, y: 4, z: 4, core: 2. Of those that a mesh axis runs over, the one named last changes fastest.
Arguments:
- grad: bfloat16 [8192, 15360], P('fsdp', 'tp'), may hold values from -6 to 6
- start_basis: bfloat16 [8192, 512], P('fsdp'), may hold values from -6 to 6
- weight: bfloat16 [8192, 15360], P('fsdp', 'tp'), may hold values from -1.1953125 to 1.1953125
- first_moment: float32 [512, 15360], P('fsdp', 'tp'), may hold values from -3 to 3
- second_moment: float32 [512, 15360], P('fsdp', 'tp'), may hold values from 0.2 to 8
Outputs:
- first_basis: bfloat16 [8192, 512], P('fsdp')
- new_basis: bfloat16 [8192, 512], P('fsdp')
- moment_one: float32 [512, 15360], P('fsdp', 'tp')
- moment_two: float32 [512, 15360], P('fsdp', 'tp')
- new_weight: bfloat16 [8192, 15360], P('fsdp', 'tp')
The draws below stay inside these ranges and needn't reach their ends.
All inputs are finite; a program needn't handle non-finite values.
Results may differ from the reference program's by a relative error of at most 0.022.
Values may be sent and summed in bfloat16 or wider, within the bound.
No kernel may reach another device: no remote copies, remote signals or barrier semaphores. Data moves between devices by JAX's collectives and lax.ppermute only.
A program may use at most 128 MiB of HBM per device.

```python
import math
import jax
import jax.numpy as jnp
from jax import lax

M = 8192
COLS = 15360
R = 512
ITERS = 2


def row_ramp(low, high):
    place = jnp.arange(M, dtype=jnp.float32) / float(M - 1)
    return (low + (high - low) * place).reshape(M, 1)


def draw_grad(key, part):
    key = jax.random.fold_in(key, 11)
    first_key = jax.random.fold_in(key, 0)
    values = jax.random.normal(first_key, (M, COLS), jnp.float32) * row_ramp(0.5, 2.0)
    return jnp.clip(values, -6.0, 6.0).astype(jnp.bfloat16)


def draw_start_basis(key, part):
    key = jax.random.fold_in(key, 23)
    values = jax.random.normal(key, (M, R), jnp.float32)
    return jnp.clip(values, -6.0, 6.0).astype(jnp.bfloat16)


def block_levels(own_key, shape, pieces, least, largest):
    factor_of = 1.0
    for axis_at, shards_of in pieces:
        heights = jax.random.uniform(jax.random.fold_in(jax.random.fold_in(own_key, 6), axis_at), (shards_of,), jnp.float32, least / len(pieces), largest / len(pieces))
        factor_of = factor_of * jnp.repeat(jnp.exp(heights), shape[axis_at] // shards_of).reshape((-1,) + (1,) * (len(shape) - 1 - axis_at))
    return factor_of


def normal_values(rng, extent, deviation, reach, pieces=(), kind=jnp.bfloat16):
    gain = block_levels(rng, extent, pieces, -0.22, 0.18) if pieces else 1.0
    entries = jax.random.normal(rng, extent, jnp.float32) * deviation * gain
    return jnp.minimum(jnp.maximum(entries, -reach), reach).astype(kind)


def setup_inputs(seed: int = 0) -> dict:
    arg_keys = jax.random.split(jax.random.key(seed), 6)
    grad = draw_grad(jax.random.fold_in(arg_keys[5], 71), 0)
    start_basis = draw_start_basis(jax.random.fold_in(arg_keys[5], 71), 0)
    weight = normal_values(arg_keys[2], (M, COLS), 0.2, 1.1953125, ((0, 16), (1, 8)))
    first_moment = normal_values(arg_keys[3], (R, COLS), 0.5, 3.0, ((0, 16), (1, 8)), jnp.float32)
    second_moment = jnp.clip(jnp.exp(math.log(8.0) - 3.6888794 * jax.random.uniform(arg_keys[4], (R, COLS), jnp.float32) ** block_levels(arg_keys[4], (R, COLS), ((0, 16), (1, 8)), -0.2, 0.2)), 0.2, 8.0)
    return {"grad": grad, "start_basis": start_basis, "weight": weight, "first_moment": first_moment, "second_moment": second_moment}


BETA_ONE = 0.9
BETA_TWO = 0.95
ADAM_EPS = 1e-06
STEP_SIZE = 2.0

def reference(grad, start_basis, weight, first_moment, second_moment):
    inv_sqrt = 1.0 / math.sqrt(M)
    basis_b = start_basis
    first_basis = start_basis
    exact = None
    for sweep in range(ITERS):
        panel_rows = (jnp.dot(grad.T.astype(jnp.float32), basis_b.astype(jnp.float32), preferred_element_type=jnp.float32) * inv_sqrt).astype(jnp.bfloat16)
        image_rows = jnp.dot(grad.astype(jnp.float32), panel_rows.astype(jnp.float32), preferred_element_type=jnp.float32)
        gram_whole = jnp.dot(image_rows.T, image_rows, precision=lax.Precision.HIGHEST) / M
        factor = jnp.linalg.cholesky(gram_whole)
        exact = lax.linalg.triangular_solve(factor, image_rows, left_side=False, lower=True, transpose_a=True)
        basis_b = exact.astype(jnp.bfloat16)
        if sweep == 0:
            first_basis = basis_b
    margin = jnp.dot(exact.T, start_basis.astype(jnp.float32), precision=lax.Precision.HIGHEST) / M
    reduced = jnp.dot(basis_b.T.astype(jnp.float32), grad.astype(jnp.float32), preferred_element_type=jnp.float32) * inv_sqrt
    moment_one = BETA_ONE * jnp.dot(margin, first_moment, precision=lax.Precision.HIGHEST) + (1.0 - BETA_ONE) * reduced
    moment_two = BETA_TWO * jnp.dot(margin * margin, second_moment, precision=lax.Precision.HIGHEST) + (1.0 - BETA_TWO) * reduced * reduced
    direction = (moment_one / (jnp.sqrt(moment_two) + ADAM_EPS)).astype(jnp.bfloat16)
    expanded = jnp.dot(basis_b.astype(jnp.float32), direction.astype(jnp.float32), preferred_element_type=jnp.float32)
    new_weight = (weight.astype(jnp.float32) - STEP_SIZE * inv_sqrt * expanded).astype(jnp.bfloat16)
    return (first_basis, basis_b, moment_one, moment_two, new_weight)
```

```python
import math

import jax
import jax.numpy as jnp
from jax import lax
from jax.experimental import pallas as pl
from jax.experimental.pallas import tpu as pltpu
from jax.sharding import PartitionSpec as P

M = 8192

BETA_ONE = 0.9
BETA_TWO = 0.95
ADAM_EPS = 1e-06
STEP_SIZE = 2.0

BF = jnp.bfloat16
F32 = jnp.float32

def elim(read, n=128):
    lane = lax.broadcasted_iota(jnp.int32, (8, n), 1)
    sub = lax.broadcasted_iota(jnp.int32, (8, n), 0)
    G = [read(g) for g in range(n // 8)]
    out = []
    for g0 in range(n // 8):
        acc = jnp.zeros((8, n), jnp.float32)
        for s0 in range(8):
            j = g0 * 8 + s0
            hit = lane == j
            r = jnp.broadcast_to(G[g0][s0:s0 + 1, :], (8, n))
            p = jnp.broadcast_to(r[:, j:j + 1], (8, n))
            row = jnp.where(lane < j, r, jnp.where(hit, 1.0, 0.0)) * lax.rsqrt(p)
            acc = jnp.where(sub == s0, row, acc)
            rr = jnp.where(hit, 1.0, r) * (1.0 / p)
            for g in range(g0, n // 8):
                c = jnp.broadcast_to(G[g][:, j:j + 1], (8, n))
                new = jnp.where(hit, 0.0, G[g]) - c * rr
                G[g] = jnp.where(sub > s0, new, G[g]) if g == g0 else new
        out.append(acc)
    return out

def dot(a, b, dims):
    return lax.dot_general(a, b, (dims, ((), ())), precision=lax.Precision.HIGHEST, preferred_element_type=jnp.float32)

NB = 128
def chol_kernel(a_ref, x_ref, w_ref, s_ref, b_ref):
    n = a_ref.shape[0]
    s_ref[...] = a_ref[...]
    b_ref[...] = jnp.zeros_like(b_ref)
    nb = n // NB
    for k in range(nb):
        lo = k * NB
        for g, v in enumerate(elim(lambda g: s_ref[pl.ds(lo + 8 * g, 8), pl.ds(lo, NB)])):
            w_ref[pl.ds(8 * g, 8), :] = v
        w = w_ref[...]
        if k:
            xk = dot(w, b_ref[lo:lo + NB, :lo], ((1,), (0,)))
            x_ref[lo:lo + NB, :lo] = xk
        x_ref[lo:lo + NB, lo:lo + NB] = w
        if lo + NB < n:
            x_ref[lo:lo + NB, lo + NB:] = jnp.zeros((NB, n - lo - NB), jnp.float32)
            hi = lo + NB
            u = dot(w, s_ref[lo:hi, hi:], ((1,), (0,)))
            s_ref[hi:, hi:] -= dot(u, u, ((0,), (0,)))
            b_ref[hi:, :hi] -= dot(u, x_ref[lo:hi, :hi], ((0,), (0,)))

def chol_inv(a):
    n = a.shape[0]
    return pl.pallas_call(
        chol_kernel,
        out_shape=jax.ShapeDtypeStruct((n, n), jnp.float32),
        in_specs=[pl.BlockSpec(memory_space=pltpu.VMEM)],
        out_specs=pl.BlockSpec(memory_space=pltpu.VMEM),
        scratch_shapes=[pltpu.VMEM((NB, NB), jnp.float32), pltpu.VMEM((n, n), jnp.float32), pltpu.VMEM((n, n), jnp.float32)],
        compiler_params=pltpu.CompilerParams(vmem_limit_bytes=32 * 2**20),
    )(a)


def mm(a, b, ca, cb):
    return lax.dot_general(a, b, (((ca,), (cb,)), ((), ())), preferred_element_type=F32)


def mm_split(a, b, ca, cb):
    hi = b.astype(BF)
    lo = (b - hi.astype(F32)).astype(BF)
    return mm(a, hi, ca, cb) + mm(a, lo, ca, cb)


def mm_split2(a, b, ca, cb):
    hi = a.astype(BF)
    lo = (a - hi.astype(F32)).astype(BF)
    return mm_split(hi, b, ca, cb) + mm(lo, b.astype(BF), ca, cb)


def scatter_sum(x, axis, n):
    parts = lax.all_to_all(x.astype(BF).reshape(n, x.shape[0] // n, x.shape[1]), axis, 0, 0, tiled=True)
    return jnp.sum(parts.astype(F32), axis=0)


def gather(x, axis, n):
    parts = lax.all_to_all(jnp.broadcast_to(x[None], (n,) + x.shape), axis, 0, 0, tiled=True)
    return parts.reshape(n * x.shape[0], x.shape[1])


def per_device(nf, nt, grad, start_basis, weight, first_moment, second_moment):
    inv_sqrt = 1.0 / math.sqrt(M)
    share_rows, cols = first_moment.shape
    share_cols = cols // nf
    rank = start_basis.shape[1]

    moments = jnp.concatenate([first_moment.astype(BF), second_moment.astype(BF)], axis=0)
    moments = moments.T.reshape(nf, share_cols, 2 * share_rows)
    moments = lax.all_to_all(moments, "fsdp", 0, 0, tiled=True).transpose(1, 0, 2)
    first_t = moments[:, :, :share_rows].reshape(share_cols, rank)
    second_t = moments[:, :, share_rows:].reshape(share_cols, rank)

    panel = (scatter_sum(mm(grad, start_basis, 0, 0), "fsdp", nf) * inv_sqrt).astype(BF)
    panel = gather(panel, "fsdp", nf)
    image = scatter_sum(mm(grad, panel, 1, 0), "tp", nt).astype(BF)
    image = lax.all_gather(image, "tp", axis=0, tiled=True)
    gram = scatter_sum(mm(image, image, 0, 0), "fsdp", nf)
    gram = lax.all_gather(gram.astype(BF), "fsdp", axis=0, tiled=True).astype(F32) / M
    inverse = chol_inv(gram)
    first_basis = mm_split(image, inverse, 1, 1).astype(BF)
    raw = scatter_sum(mm(grad, image, 0, 0), "fsdp", nf)
    panel = (mm_split2(raw, inverse, 1, 1) * inv_sqrt).astype(BF)

    panel = gather(panel, "fsdp", nf)
    image = scatter_sum(mm(grad, panel, 1, 0), "tp", nt).astype(BF)
    image = lax.all_gather(image, "tp", axis=0, tiled=True)
    both = mm(image, jnp.concatenate([image, start_basis], axis=1), 0, 0)
    both = scatter_sum(both, "fsdp", nf)
    both = lax.all_gather(both.astype(BF), "fsdp", axis=0, tiled=True)
    inverse = chol_inv(both[:, :rank].astype(F32) / M)
    margin = mm_split(both[:, rank:], inverse, 0, 1) / M
    new_basis = mm_split(image, inverse, 1, 1).astype(BF)
    raw = scatter_sum(mm(grad, image, 0, 0), "fsdp", nf)
    reduced = mm_split2(raw, inverse, 1, 1) * inv_sqrt

    rotated_one = mm(first_t, margin.astype(BF), 1, 0)
    rotated_two = mm(second_t, (margin * margin).astype(BF), 1, 0)
    moment_one = BETA_ONE * rotated_one + (1.0 - BETA_ONE) * reduced
    moment_two = BETA_TWO * rotated_two + (1.0 - BETA_TWO) * reduced * reduced
    direction = (moment_one / (jnp.sqrt(moment_two) + ADAM_EPS)).astype(BF)

    back = jnp.concatenate(
        [moment_one.astype(BF).reshape(share_cols, nf, share_rows), moment_two.astype(BF).reshape(share_cols, nf, share_rows)], axis=2
    ).transpose(1, 0, 2)
    sent = jnp.concatenate([jnp.broadcast_to(direction[None], (nf, share_cols, rank)), back], axis=2)
    got = lax.all_to_all(sent, "fsdp", 0, 0, tiled=True).reshape(cols, rank + 2 * share_rows)
    expanded = mm(new_basis, got[:, :rank], 1, 1)
    new_weight = (weight.astype(F32) - STEP_SIZE * inv_sqrt * expanded).astype(BF)
    moment_one = got[:, rank : rank + share_rows].astype(F32).T
    moment_two = got[:, rank + share_rows :].astype(F32).T
    return (first_basis, new_basis, moment_one, moment_two, new_weight)


def solution(mesh):
    specs = (P("fsdp", "tp"), P("fsdp", None), P("fsdp", "tp"), P("fsdp", "tp"), P("fsdp", "tp"))
    out_specs = (P("fsdp", None), P("fsdp", None), P("fsdp", "tp"), P("fsdp", "tp"), P("fsdp", "tp"))
    nf, nt = mesh.shape["fsdp"], mesh.shape["tp"]

    def body(*args):
        return per_device(nf, nt, *args)

    return jax.shard_map(body, mesh=mesh, in_specs=specs, out_specs=out_specs, check_vma=False)
```

```python
import math

import jax
import jax.numpy as jnp
from jax import lax
from jax.experimental import pallas as pl
from jax.experimental.pallas import tpu as pltpu
from jax.sharding import PartitionSpec as P

M = 8192

BETA_ONE = 0.9
BETA_TWO = 0.95
ADAM_EPS = 1e-06
STEP_SIZE = 2.0

BF = jnp.bfloat16
F32 = jnp.float32

def elim(read, n=128):
    lane = lax.broadcasted_iota(jnp.int32, (8, n), 1)
    sub = lax.broadcasted_iota(jnp.int32, (8, n), 0)
    G = [read(g) for g in range(n // 8)]
    out = []
    for g0 in range(n // 8):
        acc = jnp.zeros((8, n), jnp.float32)
        for s0 in range(8):
            j = g0 * 8 + s0
            hit = lane == j
            r = jnp.broadcast_to(G[g0][s0:s0 + 1, :], (8, n))
            p = jnp.broadcast_to(r[:, j:j + 1], (8, n))
            row = jnp.where(lane < j, r, jnp.where(hit, 1.0, 0.0)) * lax.rsqrt(p)
            acc = jnp.where(sub == s0, row, acc)
            rr = jnp.where(hit, 1.0, r) * (1.0 / p)
            for g in range(g0, n // 8):
                c = jnp.broadcast_to(G[g][:, j:j + 1], (8, n))
                new = jnp.where(hit, 0.0, G[g]) - c * rr
                G[g] = jnp.where(sub > s0, new, G[g]) if g == g0 else new
        out.append(acc)
    return out

def dot(a, b, dims):
    return lax.dot_general(a, b, (dims, ((), ())), precision=lax.Precision.HIGHEST, preferred_element_type=jnp.float32)

NB = 128
def chol_kernel(a_ref, x_ref, w_ref, s_ref, b_ref):
    n = a_ref.shape[0]
    s_ref[...] = a_ref[...]
    b_ref[...] = jnp.zeros_like(b_ref)
    nb = n // NB
    for k in range(nb):
        lo = k * NB
        for g, v in enumerate(elim(lambda g: s_ref[pl.ds(lo + 8 * g, 8), pl.ds(lo, NB)])):
            w_ref[pl.ds(8 * g, 8), :] = v
        w = w_ref[...]
        if k:
            xk = dot(w, b_ref[lo:lo + NB, :lo], ((1,), (0,)))
            x_ref[lo:lo + NB, :lo] = xk
        x_ref[lo:lo + NB, lo:lo + NB] = w
        if lo + NB < n:
            x_ref[lo:lo + NB, lo + NB:] = jnp.zeros((NB, n - lo - NB), jnp.float32)
            hi = lo + NB
            u = dot(w, s_ref[lo:hi, hi:], ((1,), (0,)))
            s_ref[hi:, hi:] -= dot(u, u, ((0,), (0,)))
            b_ref[hi:, :hi] -= dot(u, x_ref[lo:hi, :hi], ((0,), (0,)))

def chol_inv(a):
    n = a.shape[0]
    return pl.pallas_call(
        chol_kernel,
        out_shape=jax.ShapeDtypeStruct((n, n), jnp.float32),
        in_specs=[pl.BlockSpec(memory_space=pltpu.VMEM)],
        out_specs=pl.BlockSpec(memory_space=pltpu.VMEM),
        scratch_shapes=[pltpu.VMEM((NB, NB), jnp.float32), pltpu.VMEM((n, n), jnp.float32), pltpu.VMEM((n, n), jnp.float32)],
        cost_estimate=pl.CostEstimate(flops=60 * 10**9, bytes_accessed=2 * 2**20, transcendentals=0),
        compiler_params=pltpu.CompilerParams(vmem_limit_bytes=32 * 2**20),
    )(a)


def mm(a, b, ca, cb):
    return lax.dot_general(a, b, (((ca,), (cb,)), ((), ())), preferred_element_type=F32)


def mm_split(a, b, ca, cb):
    hi = b.astype(BF)
    lo = (b - hi.astype(F32)).astype(BF)
    return mm(a, hi, ca, cb) + mm(a, lo, ca, cb)


def mm_split2(a, b, ca, cb):
    hi = a.astype(BF)
    lo = (a - hi.astype(F32)).astype(BF)
    return mm_split(hi, b, ca, cb) + mm(lo, b.astype(BF), ca, cb)


def scatter_sum(x, axis, n):
    parts = lax.all_to_all(x.astype(BF).reshape(n, x.shape[0] // n, x.shape[1]), axis, 0, 0, tiled=True)
    return jnp.sum(parts.astype(F32), axis=0)


def gather(x, axis, n):
    parts = lax.all_to_all(jnp.broadcast_to(x[None], (n,) + x.shape), axis, 0, 0, tiled=True)
    return parts.reshape(n * x.shape[0], x.shape[1])


def per_device(nf, nt, grad, start_basis, weight, first_moment, second_moment):
    inv_sqrt = 1.0 / math.sqrt(M)
    share_rows, cols = first_moment.shape
    share_cols = cols // nf
    rank = start_basis.shape[1]

    moments = jnp.concatenate([first_moment.astype(BF), second_moment.astype(BF)], axis=0)
    moments = moments.T.reshape(nf, share_cols, 2 * share_rows)
    moments = lax.all_to_all(moments, "fsdp", 0, 0, tiled=True).transpose(1, 0, 2)
    first_t = moments[:, :, :share_rows].reshape(share_cols, rank)
    second_t = moments[:, :, share_rows:].reshape(share_cols, rank)

    panel = (scatter_sum(mm(grad, start_basis, 0, 0), "fsdp", nf) * inv_sqrt).astype(BF)
    panel = gather(panel, "fsdp", nf)
    image = scatter_sum(mm(grad, panel, 1, 0), "tp", nt).astype(BF)
    image = lax.all_gather(image, "tp", axis=0, tiled=True)
    gram = scatter_sum(mm(image, image, 0, 0), "fsdp", nf)
    gram = lax.all_gather(gram.astype(BF), "fsdp", axis=0, tiled=True)
    raw, gram = lax.optimization_barrier((mm(grad, image, 0, 0).astype(BF), gram))
    inverse = chol_inv(gram.astype(F32) / M)
    first_basis = mm_split(image, inverse, 1, 1).astype(BF)
    raw = scatter_sum(raw, "fsdp", nf)
    panel = (mm_split2(raw, inverse, 1, 1) * inv_sqrt).astype(BF)

    panel = gather(panel, "fsdp", nf)
    image = scatter_sum(mm(grad, panel, 1, 0), "tp", nt).astype(BF)
    image = lax.all_gather(image, "tp", axis=0, tiled=True)
    gram = scatter_sum(mm(image, image, 0, 0), "fsdp", nf)
    gram = lax.all_gather(gram.astype(BF), "fsdp", axis=0, tiled=True)
    raw, cross, gram = lax.optimization_barrier(
        (mm(grad, image, 0, 0).astype(BF), mm(image, start_basis, 0, 0).astype(BF), gram)
    )
    inverse = chol_inv(gram.astype(F32) / M)
    cross = scatter_sum(cross, "fsdp", nf)
    cross = gather(cross.astype(BF), "fsdp", nf)
    margin = mm_split(cross, inverse, 0, 1) / M
    new_basis = mm_split(image, inverse, 1, 1).astype(BF)
    raw = scatter_sum(raw, "fsdp", nf)
    reduced = mm_split2(raw, inverse, 1, 1) * inv_sqrt

    rotated_one = mm(first_t, margin.astype(BF), 1, 0)
    rotated_two = mm(second_t, (margin * margin).astype(BF), 1, 0)
    moment_one = BETA_ONE * rotated_one + (1.0 - BETA_ONE) * reduced
    moment_two = BETA_TWO * rotated_two + (1.0 - BETA_TWO) * reduced * reduced
    direction = (moment_one / (jnp.sqrt(moment_two) + ADAM_EPS)).astype(BF)

    back = jnp.concatenate(
        [moment_one.astype(BF).reshape(share_cols, nf, share_rows), moment_two.astype(BF).reshape(share_cols, nf, share_rows)], axis=2
    ).transpose(1, 0, 2)
    direction = gather(direction, "fsdp", nf)
    back = lax.all_to_all(back, "fsdp", 0, 0, tiled=True).reshape(cols, 2 * share_rows)
    expanded = mm(new_basis, direction, 1, 1)
    new_weight = (weight.astype(F32) - STEP_SIZE * inv_sqrt * expanded).astype(BF)
    moments = back.astype(F32).T
    moment_one, moment_two = moments[:share_rows], moments[share_rows:]
    return (first_basis, new_basis, moment_one, moment_two, new_weight)


def solution(mesh):
    specs = (P("fsdp", "tp"), P("fsdp", None), P("fsdp", "tp"), P("fsdp", "tp"), P("fsdp", "tp"))
    out_specs = (P("fsdp", None), P("fsdp", None), P("fsdp", "tp"), P("fsdp", "tp"), P("fsdp", "tp"))
    nf, nt = mesh.shape["fsdp"], mesh.shape["tp"]

    def body(*args):
        return per_device(nf, nt, *args)

    return jax.shard_map(body, mesh=mesh, in_specs=specs, out_specs=out_specs, check_vma=False)
```

```python
import math

import jax
import jax.numpy as jnp
from jax import lax
from jax.experimental import pallas as pl
from jax.experimental.pallas import tpu as pltpu
from jax.sharding import PartitionSpec as P

M = 8192

BETA_ONE = 0.9
BETA_TWO = 0.95
ADAM_EPS = 1e-06
STEP_SIZE = 2.0

BF = jnp.bfloat16
F32 = jnp.float32

def elim(read, n=128):
    lane = lax.broadcasted_iota(jnp.int32, (8, n), 1)
    sub = lax.broadcasted_iota(jnp.int32, (8, n), 0)
    G = [read(g) for g in range(n // 8)]
    out = []
    for g0 in range(n // 8):
        acc = jnp.zeros((8, n), jnp.float32)
        for s0 in range(8):
            j = g0 * 8 + s0
            hit = lane == j
            r = jnp.broadcast_to(G[g0][s0:s0 + 1, :], (8, n))
            p = jnp.broadcast_to(r[:, j:j + 1], (8, n))
            row = jnp.where(lane < j, r, jnp.where(hit, 1.0, 0.0)) * lax.rsqrt(p)
            acc = jnp.where(sub == s0, row, acc)
            rr = jnp.where(hit, 1.0, r) * (1.0 / p)
            for g in range(g0, n // 8):
                c = jnp.broadcast_to(G[g][:, j:j + 1], (8, n))
                new = jnp.where(hit, 0.0, G[g]) - c * rr
                G[g] = jnp.where(sub > s0, new, G[g]) if g == g0 else new
        out.append(acc)
    return out


NB = 128


def exact_dot(a, b, dims):
    return lax.dot_general(a, b, (dims, ((), ())), precision=lax.Precision.HIGHEST, preferred_element_type=F32)


def fast_dot(a, b, dims):
    return lax.dot_general(a, b, (dims, ((), ())), preferred_element_type=F32)


def halves(x):
    hi = x.astype(BF)
    return hi, (x - hi.astype(F32)).astype(BF)


def eliminate(a_ref, x_ref, w_ref, s_ref, b_ref):
    n = a_ref.shape[0]
    nb = n // NB
    s_ref[...] = a_ref[...]
    b_ref[...] = jnp.zeros_like(b_ref)
    x_ref[...] = jnp.zeros_like(x_ref)

    @pl.loop(0, nb)
    def _(k):
        rows = pl.ds(pl.multiple_of(k * NB, NB), NB)
        for g, v in enumerate(elim(lambda g: s_ref[pl.ds(pl.multiple_of(k * NB + 8 * g, 8), 8), rows])):
            w_ref[pl.ds(8 * g, 8), :] = v
        w = w_ref[...]
        u = exact_dot(w, s_ref[rows, :], ((1,), (0,)))
        x_ref[rows, :] = exact_dot(w, b_ref[rows, :], ((1,), (0,)))
        x_ref[rows, rows] = w

        @pl.loop(k + 1, nb)
        def _(i):
            below = pl.ds(pl.multiple_of(i * NB, NB), NB)
            ui = exact_dot(w, s_ref[rows, below], ((1,), (0,)))
            s_ref[below, :] -= exact_dot(ui, u, ((0,), (0,)))
            b_ref[below, :] -= exact_dot(ui, x_ref[rows, :], ((0,), (0,)))


def chol_kernel(a_ref, x_ref, w_ref, s_ref, b_ref, ah_ref, al_ref, yh_ref, yl_ref, e_ref, d_ref):
    n = a_ref.shape[0]
    nb = n // NB
    eye = (lax.broadcasted_iota(jnp.int32, (NB, NB), 0) == lax.broadcasted_iota(jnp.int32, (NB, NB), 1)).astype(F32)
    lower = (lax.broadcasted_iota(jnp.int32, (NB, NB), 0) > lax.broadcasted_iota(jnp.int32, (NB, NB), 1)).astype(F32) + 0.5 * eye

    for r in range(nb):
        at = pl.ds(r * NB, NB)
        d_ref[:, at] = lax.rsqrt(jnp.sum(a_ref[at, at] * eye, axis=0, keepdims=True))
    for r in range(nb):
        at = pl.ds(r * NB, NB)
        here = jnp.sum(eye * d_ref[:, at], axis=1, keepdims=True)
        hi, lo = halves(a_ref[at, :] * here * d_ref[...])
        ah_ref[at, :] = hi
        al_ref[at, :] = lo
    x_ref[...] = jnp.zeros_like(x_ref)
    for r in range(nb):
        at = pl.ds(r * NB, NB)
        end = (r + 1) * NB
        a = ah_ref[at, :end].astype(F32)
        if r:
            x_ref[at, : r * NB] = -a[:, : r * NB]
        x_ref[at, at] = eye - (a[:, r * NB :] - eye) * lower

    def step(fine):
        for r in range(nb):
            at, end = pl.ds(r * NB, NB), (r + 1) * NB
            hi, lo = halves(x_ref[at, :end])
            yh_ref[at, :end] = hi
            if fine:
                yl_ref[at, :end] = lo
        total = jnp.zeros((1, 1), F32)
        for r in range(nb):
            at, start, end = pl.ds(r * NB, NB), r * NB, (r + 1) * NB
            yh = yh_ref[at, :end]
            t = fast_dot(yh, ah_ref[:end, :end], ((1,), (0,)))
            if fine:
                t += fast_dot(yh, al_ref[:end, :end], ((1,), (0,))) + fast_dot(yl_ref[at, :end], ah_ref[:end, :end], ((1,), (0,)))
            hi, lo = halves(t)
            e = fast_dot(hi, yh_ref[:end, :end], ((1,), (1,)))
            if fine:
                e += fast_dot(lo, yh_ref[:end, :end], ((1,), (1,))) + fast_dot(hi, yl_ref[:end, :end], ((1,), (1,)))
            corner = (e[:, start:] - eye) * lower
            total += jnp.sum(corner * corner, keepdims=True)
            e_ref[at, start:end] = corner.astype(BF)
            if r:
                left = e[:, :start]
                total += jnp.sum(left * left, keepdims=True)
                e_ref[at, :start] = left.astype(BF)
        for r in reversed(range(nb)):
            at, end = pl.ds(r * NB, NB), (r + 1) * NB
            x_ref[at, :end] -= fast_dot(e_ref[at, :end], yh_ref[:end, :end], ((1,), (0,)))
        return total[0, 0]

    def more(tol, most):
        return lambda state: jnp.logical_and(state[0] < most, state[1] > tol)

    _, size = lax.while_loop(more(0.05, 10), lambda s: (s[0] + 1, step(False)), (0, jnp.float32(1e9)))
    _, size = lax.while_loop(more(1e-5, 6), lambda s: (s[0] + 1, step(True)), (0, jnp.float32(1e9)))
    good = size <= 1e-5

    @pl.when(good)
    def _():
        for r in range(nb):
            at, end = pl.ds(r * NB, NB), (r + 1) * NB
            x_ref[at, :end] *= d_ref[:, :end]

    @pl.when(jnp.logical_not(good))
    def _():
        eliminate(a_ref, x_ref, w_ref, s_ref, b_ref)


def chol_inv(a):
    n = a.shape[0]
    square = lambda kind: pltpu.VMEM((n, n), kind)
    return pl.pallas_call(
        chol_kernel,
        out_shape=jax.ShapeDtypeStruct((n, n), F32),
        in_specs=[pl.BlockSpec(memory_space=pltpu.VMEM)],
        out_specs=pl.BlockSpec(memory_space=pltpu.VMEM),
        scratch_shapes=[pltpu.VMEM((NB, NB), F32), square(F32), square(F32), square(BF), square(BF), square(BF), square(BF), square(BF), pltpu.VMEM((1, n), F32)],
        cost_estimate=pl.CostEstimate(flops=20 * 10**9, bytes_accessed=2 * 2**20, transcendentals=0),
        compiler_params=pltpu.CompilerParams(vmem_limit_bytes=32 * 2**20),
    )(a)


def mm(a, b, ca, cb):
    return lax.dot_general(a, b, (((ca,), (cb,)), ((), ())), preferred_element_type=F32)


def mm_split(a, b, ca, cb):
    hi = b.astype(BF)
    lo = (b - hi.astype(F32)).astype(BF)
    return mm(a, hi, ca, cb) + mm(a, lo, ca, cb)


def mm_split2(a, b, ca, cb):
    hi = a.astype(BF)
    lo = (a - hi.astype(F32)).astype(BF)
    return mm_split(hi, b, ca, cb) + mm(lo, b.astype(BF), ca, cb)


def scatter_sum(x, axis, n):
    parts = lax.all_to_all(x.astype(BF).reshape(n, x.shape[0] // n, x.shape[1]), axis, 0, 0, tiled=True)
    return jnp.sum(parts.astype(F32), axis=0)


def gather(x, axis, n):
    parts = lax.all_to_all(jnp.broadcast_to(x[None], (n,) + x.shape), axis, 0, 0, tiled=True)
    return parts.reshape(n * x.shape[0], x.shape[1])


def inner_sums(x, nf, nt):
    rank = x.shape[0]
    k = x.shape[1] // rank
    rows = rank // nt
    mine = lax.dynamic_slice_in_dim(x, lax.axis_index("tp") * rows, rows, 0).astype(BF)
    groups = rows // 8
    wide = nf // groups
    mine = mine.reshape(groups, 8, wide, x.shape[1] // wide).transpose(0, 2, 1, 3).reshape(nf * 8, x.shape[1] // wide)
    whole = gather(scatter_sum(mine, "fsdp", nf).astype(BF), "fsdp", nf)
    return whole.reshape(groups, wide, 8, x.shape[1] // wide).transpose(0, 2, 1, 3).reshape(rows, k * rank)


def per_device(nf, nt, grad, start_basis, weight, first_moment, second_moment):
    inv_sqrt = 1.0 / math.sqrt(M)
    share_rows, cols = first_moment.shape
    share_cols = cols // nf
    rank = start_basis.shape[1]

    moments = jnp.concatenate([first_moment.astype(BF), second_moment.astype(BF)], axis=0)
    moments = moments.T.reshape(nf, share_cols, 2 * share_rows)
    moments = lax.all_to_all(moments, "fsdp", 0, 0, tiled=True).transpose(1, 0, 2)
    first_t = moments[:, :, :share_rows].reshape(share_cols, rank)
    second_t = moments[:, :, share_rows:].reshape(share_cols, rank)

    panel = (scatter_sum(mm(grad, start_basis, 0, 0), "fsdp", nf) * inv_sqrt).astype(BF)
    panel = gather(panel, "fsdp", nf)
    image = scatter_sum(mm(grad, panel, 1, 0), "tp", nt).astype(BF)
    image = lax.all_gather(image, "tp", axis=0, tiled=True)
    gram = inner_sums(mm(image, image, 0, 0), nf, nt)
    raw, gram = lax.optimization_barrier((mm(grad, image, 0, 0).astype(BF), gram))
    gram = lax.all_gather(gram, "tp", axis=0, tiled=True)
    inverse = chol_inv(gram.astype(F32) / M)
    first_basis = mm_split(image, inverse, 1, 1).astype(BF)
    raw = scatter_sum(raw, "fsdp", nf)
    panel = (mm_split2(raw, inverse, 1, 1) * inv_sqrt).astype(BF)

    panel = gather(panel, "fsdp", nf)
    image = scatter_sum(mm(grad, panel, 1, 0), "tp", nt).astype(BF)
    image = lax.all_gather(image, "tp", axis=0, tiled=True)
    both = inner_sums(mm(image, jnp.concatenate([image, start_basis], axis=1), 0, 0), nf, nt)
    raw, both = lax.optimization_barrier((mm(grad, image, 0, 0).astype(BF), both))
    gram = lax.all_gather(both[:, :rank], "tp", axis=0, tiled=True)
    cross = lax.all_gather(both[:, rank:], "tp", axis=0, tiled=True)
    inverse = chol_inv(gram.astype(F32) / M)
    margin = mm_split(cross, inverse, 0, 1) / M
    new_basis = mm_split(image, inverse, 1, 1).astype(BF)
    raw = scatter_sum(raw, "fsdp", nf)
    reduced = mm_split2(raw, inverse, 1, 1) * inv_sqrt

    rotated_one = mm(first_t, margin.astype(BF), 1, 0)
    rotated_two = mm(second_t, (margin * margin).astype(BF), 1, 0)
    moment_one = BETA_ONE * rotated_one + (1.0 - BETA_ONE) * reduced
    moment_two = BETA_TWO * rotated_two + (1.0 - BETA_TWO) * reduced * reduced
    direction = (moment_one / (jnp.sqrt(moment_two) + ADAM_EPS)).astype(BF)

    back = jnp.concatenate(
        [moment_one.astype(BF).reshape(share_cols, nf, share_rows), moment_two.astype(BF).reshape(share_cols, nf, share_rows)], axis=2
    ).transpose(1, 0, 2)
    direction = gather(direction, "fsdp", nf)
    back = lax.all_to_all(back, "fsdp", 0, 0, tiled=True).reshape(cols, 2 * share_rows)
    expanded = mm(new_basis, direction, 1, 1)
    new_weight = (weight.astype(F32) - STEP_SIZE * inv_sqrt * expanded).astype(BF)
    moments = back.astype(F32).T
    moment_one, moment_two = moments[:share_rows], moments[share_rows:]
    return (first_basis, new_basis, moment_one, moment_two, new_weight)


def solution(mesh):
    specs = (P("fsdp", "tp"), P("fsdp", None), P("fsdp", "tp"), P("fsdp", "tp"), P("fsdp", "tp"))
    out_specs = (P("fsdp", None), P("fsdp", None), P("fsdp", "tp"), P("fsdp", "tp"), P("fsdp", "tp"))
    nf, nt = mesh.shape["fsdp"], mesh.shape["tp"]

    def body(*args):
        return per_device(nf, nt, *args)

    return jax.shard_map(body, mesh=mesh, in_specs=specs, out_specs=out_specs, check_vma=False)
```

```python
import math

import jax
import jax.numpy as jnp
from jax import lax
from jax.experimental import pallas as pl
from jax.experimental.pallas import tpu as pltpu
from jax.sharding import PartitionSpec as P

M = 8192

BETA_ONE = 0.9
BETA_TWO = 0.95
ADAM_EPS = 1e-06
STEP_SIZE = 2.0

BF = jnp.bfloat16
F32 = jnp.float32

def elim(read, n=128):
    lane = lax.broadcasted_iota(jnp.int32, (8, n), 1)
    sub = lax.broadcasted_iota(jnp.int32, (8, n), 0)
    G = [read(g) for g in range(n // 8)]
    out = []
    for g0 in range(n // 8):
        acc = jnp.zeros((8, n), jnp.float32)
        for s0 in range(8):
            j = g0 * 8 + s0
            hit = lane == j
            r = jnp.broadcast_to(G[g0][s0:s0 + 1, :], (8, n))
            p = jnp.broadcast_to(r[:, j:j + 1], (8, n))
            row = jnp.where(lane < j, r, jnp.where(hit, 1.0, 0.0)) * lax.rsqrt(p)
            acc = jnp.where(sub == s0, row, acc)
            rr = jnp.where(hit, 1.0, r) * (1.0 / p)
            for g in range(g0, n // 8):
                c = jnp.broadcast_to(G[g][:, j:j + 1], (8, n))
                new = jnp.where(hit, 0.0, G[g]) - c * rr
                G[g] = jnp.where(sub > s0, new, G[g]) if g == g0 else new
        out.append(acc)
    return out


NB = 128


def exact_dot(a, b, dims):
    return lax.dot_general(a, b, (dims, ((), ())), precision=lax.Precision.HIGHEST, preferred_element_type=F32)


def fast_dot(a, b, dims):
    return lax.dot_general(a, b, (dims, ((), ())), preferred_element_type=F32)


def halves(x):
    hi = x.astype(BF)
    return hi, (x - hi.astype(F32)).astype(BF)


def eliminate(a_ref, x_ref, w_ref, s_ref, b_ref):
    n = a_ref.shape[0]
    nb = n // NB
    s_ref[...] = a_ref[...]
    b_ref[...] = jnp.zeros_like(b_ref)
    x_ref[...] = jnp.zeros_like(x_ref)

    @pl.loop(0, nb)
    def _(k):
        rows = pl.ds(pl.multiple_of(k * NB, NB), NB)
        for g, v in enumerate(elim(lambda g: s_ref[pl.ds(pl.multiple_of(k * NB + 8 * g, 8), 8), rows])):
            w_ref[pl.ds(8 * g, 8), :] = v
        w = w_ref[...]
        u = exact_dot(w, s_ref[rows, :], ((1,), (0,)))
        x_ref[rows, :] = exact_dot(w, b_ref[rows, :], ((1,), (0,)))
        x_ref[rows, rows] = w

        @pl.loop(k + 1, nb)
        def _(i):
            below = pl.ds(pl.multiple_of(i * NB, NB), NB)
            ui = exact_dot(w, s_ref[rows, below], ((1,), (0,)))
            s_ref[below, :] -= exact_dot(ui, u, ((0,), (0,)))
            b_ref[below, :] -= exact_dot(ui, x_ref[rows, :], ((0,), (0,)))


def chol_kernel(a_ref, x_ref, w_ref, s_ref, b_ref, ah_ref, al_ref, yh_ref, yl_ref, e_ref, d_ref):
    n = a_ref.shape[0]
    nb = n // NB
    eye = (lax.broadcasted_iota(jnp.int32, (NB, NB), 0) == lax.broadcasted_iota(jnp.int32, (NB, NB), 1)).astype(F32)
    lower = (lax.broadcasted_iota(jnp.int32, (NB, NB), 0) > lax.broadcasted_iota(jnp.int32, (NB, NB), 1)).astype(F32) + 0.5 * eye

    for r in range(nb):
        at = pl.ds(r * NB, NB)
        d_ref[:, at] = lax.rsqrt(jnp.sum(a_ref[at, at] * eye, axis=0, keepdims=True))
    for r in range(nb):
        at = pl.ds(r * NB, NB)
        here = jnp.sum(eye * d_ref[:, at], axis=1, keepdims=True)
        hi, lo = halves(a_ref[at, :] * here * d_ref[...])
        ah_ref[at, :] = hi
        al_ref[at, :] = lo
    x_ref[...] = jnp.zeros_like(x_ref)
    yh_ref[...] = jnp.zeros_like(yh_ref)
    yl_ref[...] = jnp.zeros_like(yl_ref)
    for r in range(nb):
        at = pl.ds(r * NB, NB)
        end = (r + 1) * NB
        a = ah_ref[at, :end].astype(F32)
        if r:
            x_ref[at, : r * NB] = -a[:, : r * NB]
        x_ref[at, at] = eye - (a[:, r * NB :] - eye) * lower

    def step(fine):
        for r in range(nb):
            at, end = pl.ds(r * NB, NB), (r + 1) * NB
            hi, lo = halves(x_ref[at, :end])
            yh_ref[at, :end] = hi
            if fine:
                yl_ref[at, :end] = lo
        total = jnp.zeros((1, 1), F32)
        for r in range(nb):
            at, start, end = pl.ds(r * NB, NB), r * NB, (r + 1) * NB
            yh = yh_ref[at, :end]
            t = fast_dot(yh, ah_ref[:end, :end], ((1,), (0,)))
            if fine:
                t += fast_dot(yh, al_ref[:end, :end], ((1,), (0,))) + fast_dot(yl_ref[at, :end], ah_ref[:end, :end], ((1,), (0,)))
            hi, lo = halves(t)
            e = fast_dot(hi, yh_ref[:end, :end], ((1,), (1,)))
            if fine:
                e += fast_dot(lo, yh_ref[:end, :end], ((1,), (1,))) + fast_dot(hi, yl_ref[:end, :end], ((1,), (1,)))
            corner = (e[:, start:] - eye) * lower
            total += jnp.sum(corner * corner, keepdims=True)
            e_ref[at, start:end] = corner.astype(BF)
            if r:
                left = e[:, :start]
                total += jnp.sum(left * left, keepdims=True)
                e_ref[at, :start] = left.astype(BF)
        for r in reversed(range(nb)):
            at, end = pl.ds(r * NB, NB), (r + 1) * NB
            x_ref[at, :end] -= fast_dot(e_ref[at, :end], yh_ref[:end, :end], ((1,), (0,)))
        return total[0, 0]

    def more(tol, most):
        return lambda state: jnp.logical_and(state[0] < most, state[1] > tol)

    _, size = lax.while_loop(more(0.05, 10), lambda s: (s[0] + 1, step(False)), (0, jnp.float32(1e9)))
    _, size = lax.while_loop(more(1e-5, 6), lambda s: (s[0] + 1, step(True)), (0, jnp.float32(1e9)))
    good = size <= 1e-5

    @pl.when(good)
    def _():
        for r in range(nb):
            at, end = pl.ds(r * NB, NB), (r + 1) * NB
            x_ref[at, :end] *= d_ref[:, :end]

    @pl.when(jnp.logical_not(good))
    def _():
        eliminate(a_ref, x_ref, w_ref, s_ref, b_ref)


def chol_inv(a):
    n = a.shape[0]
    square = lambda kind: pltpu.VMEM((n, n), kind)
    return pl.pallas_call(
        chol_kernel,
        out_shape=jax.ShapeDtypeStruct((n, n), F32),
        in_specs=[pl.BlockSpec(memory_space=pltpu.VMEM)],
        out_specs=pl.BlockSpec(memory_space=pltpu.VMEM),
        scratch_shapes=[pltpu.VMEM((NB, NB), F32), square(F32), square(F32), square(BF), square(BF), square(BF), square(BF), square(BF), pltpu.VMEM((1, n), F32)],
        cost_estimate=pl.CostEstimate(flops=10**9, bytes_accessed=2 * 2**20, transcendentals=0),
        compiler_params=pltpu.CompilerParams(vmem_limit_bytes=32 * 2**20),
    )(a)


def mm(a, b, ca, cb):
    return lax.dot_general(a, b, (((ca,), (cb,)), ((), ())), preferred_element_type=F32)


def mm_split(a, b, ca, cb):
    hi = b.astype(BF)
    lo = (b - hi.astype(F32)).astype(BF)
    return mm(a, hi, ca, cb) + mm(a, lo, ca, cb)


def mm_split2(a, b, ca, cb):
    hi = a.astype(BF)
    lo = (a - hi.astype(F32)).astype(BF)
    return mm_split(hi, b, ca, cb) + mm(lo, b.astype(BF), ca, cb)


def scatter_sum(x, axis, n):
    parts = lax.all_to_all(x.astype(BF).reshape(n, x.shape[0] // n, x.shape[1]), axis, 0, 0, tiled=True)
    return jnp.sum(parts.astype(F32), axis=0)


def gather(x, axis, n):
    parts = lax.all_to_all(jnp.broadcast_to(x[None], (n,) + x.shape), axis, 0, 0, tiled=True)
    return parts.reshape(n * x.shape[0], x.shape[1])


def inner_sums(x, raw, nf, nt):
    rank = x.shape[0]
    k = x.shape[1] // rank
    rows = rank // nt
    mine = lax.dynamic_slice_in_dim(x, lax.axis_index("tp") * rows, rows, 0).astype(BF)
    groups = rows // 8
    wide = nf // groups
    mine = mine.reshape(groups, 8, wide, x.shape[1] // wide).transpose(0, 2, 1, 3).reshape(nf * 8, x.shape[1] // wide)
    sums, raw = lax.optimization_barrier((scatter_sum(mine, "fsdp", nf).astype(BF), raw))
    whole = lax.all_gather(sums, "fsdp", axis=0, tiled=True)
    return whole.reshape(groups, wide, 8, x.shape[1] // wide).transpose(0, 2, 1, 3).reshape(rows, k * rank), raw


def per_device(nf, nt, grad, start_basis, weight, first_moment, second_moment):
    inv_sqrt = 1.0 / math.sqrt(M)
    share_rows, cols = first_moment.shape
    share_cols = cols // nf
    rank = start_basis.shape[1]

    moments = jnp.concatenate([first_moment.astype(BF), second_moment.astype(BF)], axis=0)
    moments = moments.T.reshape(nf, share_cols, 2 * share_rows)
    moments = lax.all_to_all(moments, "fsdp", 0, 0, tiled=True).transpose(1, 0, 2)
    first_t = moments[:, :, :share_rows].reshape(share_cols, rank)
    second_t = moments[:, :, share_rows:].reshape(share_cols, rank)

    panel = (scatter_sum(mm(grad, start_basis, 0, 0), "fsdp", nf) * inv_sqrt).astype(BF)
    panel = gather(panel, "fsdp", nf)
    image = scatter_sum(mm(grad, panel, 1, 0), "tp", nt).astype(BF)
    image = lax.all_gather(image, "tp", axis=0, tiled=True)
    gram, raw = inner_sums(mm(image, image, 0, 0), mm(grad, image, 0, 0).astype(BF), nf, nt)
    gram = lax.all_gather(gram, "tp", axis=0, tiled=True)
    inverse = chol_inv(gram.astype(F32) / M)
    first_basis = mm_split(image, inverse, 1, 1).astype(BF)
    raw = scatter_sum(raw, "fsdp", nf)
    panel = (mm_split2(raw, inverse, 1, 1) * inv_sqrt).astype(BF)

    panel = gather(panel, "fsdp", nf)
    image = scatter_sum(mm(grad, panel, 1, 0), "tp", nt).astype(BF)
    image = lax.all_gather(image, "tp", axis=0, tiled=True)
    both = mm(image, jnp.concatenate([image, start_basis], axis=1), 0, 0)
    both, raw = inner_sums(both, mm(grad, image, 0, 0).astype(BF), nf, nt)
    gram = lax.all_gather(both[:, :rank], "tp", axis=0, tiled=True)
    cross = lax.all_gather(both[:, rank:], "tp", axis=0, tiled=True)
    inverse = chol_inv(gram.astype(F32) / M)
    margin = mm_split(cross, inverse, 0, 1) / M
    new_basis = mm_split(image, inverse, 1, 1).astype(BF)
    raw = scatter_sum(raw, "fsdp", nf)
    reduced = mm_split2(raw, inverse, 1, 1) * inv_sqrt

    rotated_one = mm(first_t, margin.astype(BF), 1, 0)
    rotated_two = mm(second_t, (margin * margin).astype(BF), 1, 0)
    moment_one = BETA_ONE * rotated_one + (1.0 - BETA_ONE) * reduced
    moment_two = BETA_TWO * rotated_two + (1.0 - BETA_TWO) * reduced * reduced
    direction = (moment_one / (jnp.sqrt(moment_two) + ADAM_EPS)).astype(BF)

    back = jnp.stack([moment_one.astype(BF), moment_two.astype(BF)], axis=1)
    back = back.reshape(share_cols, 2, nf, share_rows).transpose(2, 0, 1, 3).reshape(nf, share_cols, 2 * share_rows)
    back = jnp.pad(back, ((0, 0), (0, 0), (0, -2 * share_rows % 128)))
    sent = jnp.concatenate([jnp.broadcast_to(direction[None], (nf, share_cols, rank)), back], axis=2)
    got = lax.all_to_all(sent, "fsdp", 0, 0, tiled=True).reshape(cols, sent.shape[2])
    expanded = mm(new_basis, got[:, :rank], 1, 1)
    new_weight = (weight.astype(F32) - STEP_SIZE * inv_sqrt * expanded).astype(BF)
    moments = got[:, rank : rank + 2 * share_rows].astype(F32).T
    moment_one, moment_two = moments[:share_rows], moments[share_rows:]
    return (first_basis, new_basis, moment_one, moment_two, new_weight)


def solution(mesh):
    specs = (P("fsdp", "tp"), P("fsdp", None), P("fsdp", "tp"), P("fsdp", "tp"), P("fsdp", "tp"))
    out_specs = (P("fsdp", None), P("fsdp", None), P("fsdp", "tp"), P("fsdp", "tp"), P("fsdp", "tp"))
    nf, nt = mesh.shape["fsdp"], mesh.shape["tp"]

    def body(*args):
        return per_device(nf, nt, *args)

    return jax.shard_map(body, mesh=mesh, in_specs=specs, out_specs=out_specs, check_vma=False)
```

```python
import functools
import math

import jax
import jax.numpy as jnp
from jax import lax
from jax.experimental import pallas as pl
from jax.experimental.pallas import tpu as pltpu
from jax.experimental.layout import Layout, with_layout_constraint
from jax.sharding import PartitionSpec as P

M = 8192

BETA_ONE = 0.9
BETA_TWO = 0.95
ADAM_EPS = 1e-06
STEP_SIZE = 2.0

BF = jnp.bfloat16
F32 = jnp.float32

def elim(read, n=128):
    lane = lax.broadcasted_iota(jnp.int32, (8, n), 1)
    sub = lax.broadcasted_iota(jnp.int32, (8, n), 0)
    G = [read(g) for g in range(n // 8)]
    out = []
    for g0 in range(n // 8):
        acc = jnp.zeros((8, n), jnp.float32)
        for s0 in range(8):
            j = g0 * 8 + s0
            hit = lane == j
            r = jnp.broadcast_to(G[g0][s0:s0 + 1, :], (8, n))
            p = jnp.broadcast_to(r[:, j:j + 1], (8, n))
            row = jnp.where(lane < j, r, jnp.where(hit, 1.0, 0.0)) * lax.rsqrt(p)
            acc = jnp.where(sub == s0, row, acc)
            rr = jnp.where(hit, 1.0, r) * (1.0 / p)
            for g in range(g0, n // 8):
                c = jnp.broadcast_to(G[g][:, j:j + 1], (8, n))
                new = jnp.where(hit, 0.0, G[g]) - c * rr
                G[g] = jnp.where(sub > s0, new, G[g]) if g == g0 else new
        out.append(acc)
    return out


NB = 128


def exact_dot(a, b, dims):
    return lax.dot_general(a, b, (dims, ((), ())), precision=lax.Precision.HIGHEST, preferred_element_type=F32)


def fast_dot(a, b, dims):
    return lax.dot_general(a, b, (dims, ((), ())), preferred_element_type=F32)


def halves(x):
    hi = x.astype(BF)
    return hi, (x - hi.astype(F32)).astype(BF)


def eliminate(a_ref, x_ref, w_ref, s_ref, b_ref):
    n = a_ref.shape[0]
    nb = n // NB
    s_ref[...] = a_ref[...]
    b_ref[...] = jnp.zeros_like(b_ref)
    x_ref[...] = jnp.zeros_like(x_ref)

    @pl.loop(0, nb)
    def _(k):
        rows = pl.ds(pl.multiple_of(k * NB, NB), NB)
        for g, v in enumerate(elim(lambda g: s_ref[pl.ds(pl.multiple_of(k * NB + 8 * g, 8), 8), rows])):
            w_ref[pl.ds(8 * g, 8), :] = v
        w = w_ref[...]
        u = exact_dot(w, s_ref[rows, :], ((1,), (0,)))
        x_ref[rows, :] = exact_dot(w, b_ref[rows, :], ((1,), (0,)))
        x_ref[rows, rows] = w

        @pl.loop(k + 1, nb)
        def _(i):
            below = pl.ds(pl.multiple_of(i * NB, NB), NB)
            ui = exact_dot(w, s_ref[rows, below], ((1,), (0,)))
            s_ref[below, :] -= exact_dot(ui, u, ((0,), (0,)))
            b_ref[below, :] -= exact_dot(ui, x_ref[rows, :], ((0,), (0,)))


def chol_kernel(a_ref, x_ref, w_ref, s_ref, b_ref, ah_ref, al_ref, yh_ref, yl_ref, e_ref, d_ref):
    n = a_ref.shape[0]
    nb = n // NB
    eye = (lax.broadcasted_iota(jnp.int32, (NB, NB), 0) == lax.broadcasted_iota(jnp.int32, (NB, NB), 1)).astype(F32)
    lower = (lax.broadcasted_iota(jnp.int32, (NB, NB), 0) > lax.broadcasted_iota(jnp.int32, (NB, NB), 1)).astype(F32) + 0.5 * eye

    for r in range(nb):
        at = pl.ds(r * NB, NB)
        d_ref[:, at] = lax.rsqrt(jnp.sum(a_ref[at, at] * eye, axis=0, keepdims=True))
    for r in range(nb):
        at = pl.ds(r * NB, NB)
        here = jnp.sum(eye * d_ref[:, at], axis=1, keepdims=True)
        hi, lo = halves(a_ref[at, :] * here * d_ref[...])
        ah_ref[at, :] = hi
        al_ref[at, :] = lo
    x_ref[...] = jnp.zeros_like(x_ref)
    yh_ref[...] = jnp.zeros_like(yh_ref)
    yl_ref[...] = jnp.zeros_like(yl_ref)
    for r in range(nb):
        at = pl.ds(r * NB, NB)
        end = (r + 1) * NB
        a = ah_ref[at, :end].astype(F32)
        if r:
            x_ref[at, : r * NB] = -a[:, : r * NB]
        x_ref[at, at] = eye - (a[:, r * NB :] - eye) * lower

    def step(fine):
        for r in range(nb):
            at, end = pl.ds(r * NB, NB), (r + 1) * NB
            hi, lo = halves(x_ref[at, :end])
            yh_ref[at, :end] = hi
            if fine:
                yl_ref[at, :end] = lo
        total = jnp.zeros((1, 1), F32)
        for r in range(nb):
            at, start, end = pl.ds(r * NB, NB), r * NB, (r + 1) * NB
            yh = yh_ref[at, :end]
            t = fast_dot(yh, ah_ref[:end, :end], ((1,), (0,)))
            if fine:
                t += fast_dot(yh, al_ref[:end, :end], ((1,), (0,))) + fast_dot(yl_ref[at, :end], ah_ref[:end, :end], ((1,), (0,)))
            hi, lo = halves(t)
            e = fast_dot(hi, yh_ref[:end, :end], ((1,), (1,)))
            if fine:
                e += fast_dot(lo, yh_ref[:end, :end], ((1,), (1,))) + fast_dot(hi, yl_ref[:end, :end], ((1,), (1,)))
            corner = (e[:, start:] - eye) * lower
            total += jnp.sum(corner * corner, keepdims=True)
            e_ref[at, start:end] = corner.astype(BF)
            if r:
                left = e[:, :start]
                total += jnp.sum(left * left, keepdims=True)
                e_ref[at, :start] = left.astype(BF)
        for r in reversed(range(nb)):
            at, end = pl.ds(r * NB, NB), (r + 1) * NB
            x_ref[at, :end] -= fast_dot(e_ref[at, :end], yh_ref[:end, :end], ((1,), (0,)))
        return total[0, 0]

    def more(tol, most):
        return lambda state: jnp.logical_and(state[0] < most, state[1] > tol)

    _, size = lax.while_loop(more(0.05, 10), lambda s: (s[0] + 1, step(False)), (0, jnp.float32(1e9)))
    _, size = lax.while_loop(more(1e-5, 6), lambda s: (s[0] + 1, step(True)), (0, jnp.float32(1e9)))
    good = size <= 1e-5

    @pl.when(good)
    def _():
        for r in range(nb):
            at, end = pl.ds(r * NB, NB), (r + 1) * NB
            x_ref[at, :end] *= d_ref[:, :end]

    @pl.when(jnp.logical_not(good))
    def _():
        eliminate(a_ref, x_ref, w_ref, s_ref, b_ref)


def chol_inv(a):
    n = a.shape[0]
    square = lambda kind: pltpu.VMEM((n, n), kind)
    return pl.pallas_call(
        chol_kernel,
        out_shape=jax.ShapeDtypeStruct((n, n), F32),
        in_specs=[pl.BlockSpec(memory_space=pltpu.VMEM)],
        out_specs=pl.BlockSpec(memory_space=pltpu.VMEM),
        scratch_shapes=[pltpu.VMEM((NB, NB), F32), square(F32), square(F32), square(BF), square(BF), square(BF), square(BF), square(BF), pltpu.VMEM((1, n), F32)],
        cost_estimate=pl.CostEstimate(flops=10**9, bytes_accessed=2 * 2**20, transcendentals=0),
        compiler_params=pltpu.CompilerParams(vmem_limit_bytes=32 * 2**20),
    )(a)


def mm(a, b, ca, cb):
    return lax.dot_general(a, b, (((ca,), (cb,)), ((), ())), preferred_element_type=F32)


def mm_split(a, b, ca, cb):
    hi = b.astype(BF)
    lo = (b - hi.astype(F32)).astype(BF)
    return mm(a, hi, ca, cb) + mm(a, lo, ca, cb)


def mm_split2(a, b, ca, cb):
    hi = a.astype(BF)
    lo = (a - hi.astype(F32)).astype(BF)
    return mm_split(hi, b, ca, cb) + mm(lo, b.astype(BF), ca, cb)


def scatter_sum(x, axis, n):
    parts = lax.all_to_all(x.astype(BF).reshape(n, x.shape[0] // n, x.shape[1]), axis, 0, 0, tiled=True)
    return jnp.sum(parts.astype(F32), axis=0)


def gather(x, axis, n):
    parts = lax.all_to_all(jnp.broadcast_to(x[None], (n,) + x.shape), axis, 0, 0, tiled=True)
    return parts.reshape(n * x.shape[0], x.shape[1])


def row_major(x):
    return with_layout_constraint(x, Layout(tuple(range(x.ndim))))


def chunks(x, nf, nt):
    rows = x.shape[0] // nt
    mine = lax.dynamic_slice_in_dim(x, lax.axis_index("tp") * rows, rows, 0).astype(BF)
    return mine.reshape(rows // 8, 8, x.shape[1] // 128, 128).transpose(0, 2, 1, 3).reshape(nf, -1, 128)


def unchunk(parts, nf, rows):
    whole = gather(jnp.sum(parts.astype(F32), axis=0).astype(BF), "fsdp", nf)
    return whole.reshape(rows // 8, -1, 8, 128).transpose(0, 2, 1, 3).reshape(rows, -1)


def finish_kernel(scale, parts_ref, high_ref, low_ref, one_ref, two_ref, out_ref):
    nf, rows, rank = parts_ref.shape
    share = rank // nf
    raw = parts_ref[0].astype(F32)
    for g in range(1, nf):
        raw += parts_ref[g].astype(F32)
    hi, lo = halves(raw)
    dims = ((1,), (1,))
    reduced = (fast_dot(hi, high_ref[...], dims) + fast_dot(lo, high_ref[...], dims) + fast_dot(hi, low_ref[...], dims)) * scale
    one = BETA_ONE * one_ref[...] + (1.0 - BETA_ONE) * reduced
    two = BETA_TWO * two_ref[...] + (1.0 - BETA_TWO) * reduced * reduced
    direction = (one / (jnp.sqrt(two) + ADAM_EPS)).astype(BF)
    fill = jnp.zeros((rows, out_ref.shape[2] - rank - 2 * share), F32)
    for g in range(nf):
        out_ref[g, :, :rank] = direction
        at = slice(g * share, (g + 1) * share)
        out_ref[g, :, rank:] = jnp.concatenate([one[:, at], two[:, at], fill], axis=1).astype(BF)


def finish(scale, parts, high, low, one, two):
    nf, rows, rank = parts.shape
    width = rank + 2 * rank // nf
    width += -width % 128
    return pl.pallas_call(
        functools.partial(finish_kernel, scale),
        out_shape=jax.ShapeDtypeStruct((nf, rows, width), BF),
        in_specs=[pl.BlockSpec(memory_space=pltpu.VMEM)] * 5,
        out_specs=pl.BlockSpec(memory_space=pltpu.VMEM),
        cost_estimate=pl.CostEstimate(flops=10**9, bytes_accessed=6 * 2**20, transcendentals=0),
        compiler_params=pltpu.CompilerParams(vmem_limit_bytes=32 * 2**20),
    )(parts, high, low, one, two)


def per_device(nf, nt, grad, start_basis, weight, first_moment, second_moment):
    inv_sqrt = 1.0 / math.sqrt(M)
    share_rows, cols = first_moment.shape
    share_cols = cols // nf
    rank = start_basis.shape[1]

    sent = jnp.concatenate([first_moment.astype(BF), second_moment.astype(BF)], axis=0)
    sent = sent.reshape(2 * share_rows, nf, share_cols).transpose(1, 0, 2)
    sent = row_major(jnp.pad(sent, ((0, 0), (0, 0), (0, -share_cols % 128))))

    panel = (scatter_sum(mm(grad, start_basis, 0, 0), "fsdp", nf) * inv_sqrt).astype(BF)
    panel = gather(panel, "fsdp", nf)
    image = scatter_sum(mm(grad, panel, 1, 0), "tp", nt).astype(BF)
    image = lax.all_gather(image, "tp", axis=0, tiled=True)
    raw = row_major(mm(grad, image, 0, 0).astype(BF))
    rows = rank // nt
    got = jnp.concatenate([sent, chunks(mm(image, image, 0, 0), nf, nt)], axis=1)
    got = lax.all_to_all(got, "fsdp", 0, 0, tiled=True)
    first_old = got[:, :share_rows].reshape(rank, -1)
    second_old = got[:, share_rows : 2 * share_rows].reshape(rank, -1)
    gram, raw = lax.optimization_barrier((unchunk(got[:, 2 * share_rows :], nf, rows), raw))
    gram = lax.all_gather(gram, "tp", axis=0, tiled=True)
    inverse = chol_inv(gram.astype(F32) / M)
    first_basis = mm_split(image, inverse, 1, 1).astype(BF)
    raw = scatter_sum(raw, "fsdp", nf)
    panel = (mm_split2(raw, inverse, 1, 1) * inv_sqrt).astype(BF)

    panel = gather(panel, "fsdp", nf)
    image = scatter_sum(mm(grad, panel, 1, 0), "tp", nt).astype(BF)
    image = lax.all_gather(image, "tp", axis=0, tiled=True)
    raw = row_major(mm(grad, image, 0, 0).astype(BF))
    both = chunks(mm(image, jnp.concatenate([image, start_basis], axis=1), 0, 0), nf, nt)
    both = unchunk(lax.all_to_all(both, "fsdp", 0, 0, tiled=True), nf, rows)
    both, raw = lax.optimization_barrier((both, raw))
    gram = lax.all_gather(both[:, :rank], "tp", axis=0, tiled=True)
    cross = lax.all_gather(both[:, rank:], "tp", axis=0, tiled=True)
    inverse = chol_inv(gram.astype(F32) / M)
    margin = mm_split(cross, inverse, 0, 1) / M
    new_basis = mm_split(image, inverse, 1, 1).astype(BF)
    rotated_one = mm(first_old, margin.astype(BF), 0, 0)[:share_cols]
    rotated_two = mm(second_old, (margin * margin).astype(BF), 0, 0)[:share_cols]
    parts = lax.all_to_all(raw.reshape(nf, share_cols, rank), "fsdp", 0, 0, tiled=True)
    sent = finish(inv_sqrt, parts, *halves(inverse), rotated_one, rotated_two)
    got = lax.all_to_all(sent, "fsdp", 0, 0, tiled=True).reshape(cols, sent.shape[2])
    expanded = mm(new_basis, got[:, :rank], 1, 1)
    new_weight = (weight.astype(F32) - STEP_SIZE * inv_sqrt * expanded).astype(BF)
    eye = jnp.eye(share_rows, dtype=BF)
    moment_one = mm(eye, got[:, rank : rank + share_rows], 1, 1)
    moment_two = mm(eye, got[:, rank + share_rows : rank + 2 * share_rows], 1, 1)
    return (first_basis, new_basis, moment_one, moment_two, new_weight)


def solution(mesh):
    specs = (P("fsdp", "tp"), P("fsdp", None), P("fsdp", "tp"), P("fsdp", "tp"), P("fsdp", "tp"))
    out_specs = (P("fsdp", None), P("fsdp", None), P("fsdp", "tp"), P("fsdp", "tp"), P("fsdp", "tp"))
    nf, nt = mesh.shape["fsdp"], mesh.shape["tp"]

    def body(*args):
        return per_device(nf, nt, *args)

    return jax.shard_map(body, mesh=mesh, in_specs=specs, out_specs=out_specs, check_vma=False)
```

```python
import functools
import math

import jax
import jax.numpy as jnp
from jax import lax
from jax.experimental import pallas as pl
from jax.experimental.pallas import tpu as pltpu
from jax.experimental.layout import Layout, with_layout_constraint
from jax.sharding import PartitionSpec as P

M = 8192

BETA_ONE = 0.9
BETA_TWO = 0.95
ADAM_EPS = 1e-06
STEP_SIZE = 2.0

BF = jnp.bfloat16
F32 = jnp.float32

def elim(read, n=128):
    lane = lax.broadcasted_iota(jnp.int32, (8, n), 1)
    sub = lax.broadcasted_iota(jnp.int32, (8, n), 0)
    G = [read(g) for g in range(n // 8)]
    out = []
    for g0 in range(n // 8):
        acc = jnp.zeros((8, n), jnp.float32)
        for s0 in range(8):
            j = g0 * 8 + s0
            hit = lane == j
            r = jnp.broadcast_to(G[g0][s0:s0 + 1, :], (8, n))
            p = jnp.broadcast_to(r[:, j:j + 1], (8, n))
            row = jnp.where(lane < j, r, jnp.where(hit, 1.0, 0.0)) * lax.rsqrt(p)
            acc = jnp.where(sub == s0, row, acc)
            rr = jnp.where(hit, 1.0, r) * (1.0 / p)
            for g in range(g0, n // 8):
                c = jnp.broadcast_to(G[g][:, j:j + 1], (8, n))
                new = jnp.where(hit, 0.0, G[g]) - c * rr
                G[g] = jnp.where(sub > s0, new, G[g]) if g == g0 else new
        out.append(acc)
    return out


NB = 128


def exact_dot(a, b, dims):
    return lax.dot_general(a, b, (dims, ((), ())), precision=lax.Precision.HIGHEST, preferred_element_type=F32)


def fast_dot(a, b, dims):
    return lax.dot_general(a, b, (dims, ((), ())), preferred_element_type=F32)


def halves(x):
    hi = x.astype(BF)
    return hi, (x - hi.astype(F32)).astype(BF)


def eliminate(a_ref, x_ref, w_ref, s_ref, b_ref):
    n = a_ref.shape[0]
    nb = n // NB
    s_ref[...] = a_ref[...]
    b_ref[...] = jnp.zeros_like(b_ref)
    x_ref[...] = jnp.zeros_like(x_ref)

    @pl.loop(0, nb)
    def _(k):
        rows = pl.ds(pl.multiple_of(k * NB, NB), NB)
        for g, v in enumerate(elim(lambda g: s_ref[pl.ds(pl.multiple_of(k * NB + 8 * g, 8), 8), rows])):
            w_ref[pl.ds(8 * g, 8), :] = v
        w = w_ref[...]
        u = exact_dot(w, s_ref[rows, :], ((1,), (0,)))
        x_ref[rows, :] = exact_dot(w, b_ref[rows, :], ((1,), (0,)))
        x_ref[rows, rows] = w

        @pl.loop(k + 1, nb)
        def _(i):
            below = pl.ds(pl.multiple_of(i * NB, NB), NB)
            ui = exact_dot(w, s_ref[rows, below], ((1,), (0,)))
            s_ref[below, :] -= exact_dot(ui, u, ((0,), (0,)))
            b_ref[below, :] -= exact_dot(ui, x_ref[rows, :], ((0,), (0,)))


def chol_kernel(a_ref, x_ref, w_ref, s_ref, b_ref, ah_ref, al_ref, yh_ref, yl_ref, e_ref, d_ref):
    n = a_ref.shape[0]
    nb = n // NB
    eye = (lax.broadcasted_iota(jnp.int32, (NB, NB), 0) == lax.broadcasted_iota(jnp.int32, (NB, NB), 1)).astype(F32)
    lower = (lax.broadcasted_iota(jnp.int32, (NB, NB), 0) > lax.broadcasted_iota(jnp.int32, (NB, NB), 1)).astype(F32) + 0.5 * eye

    for r in range(nb):
        at = pl.ds(r * NB, NB)
        d_ref[:, at] = lax.rsqrt(jnp.sum(a_ref[at, at] * eye, axis=0, keepdims=True))
    for r in range(nb):
        at = pl.ds(r * NB, NB)
        here = jnp.sum(eye * d_ref[:, at], axis=1, keepdims=True)
        hi, lo = halves(a_ref[at, :] * here * d_ref[...])
        ah_ref[at, :] = hi
        al_ref[at, :] = lo
    x_ref[...] = jnp.zeros_like(x_ref)
    yh_ref[...] = jnp.zeros_like(yh_ref)
    yl_ref[...] = jnp.zeros_like(yl_ref)
    for r in range(nb):
        at = pl.ds(r * NB, NB)
        end = (r + 1) * NB
        a = ah_ref[at, :end].astype(F32)
        if r:
            x_ref[at, : r * NB] = -a[:, : r * NB]
        x_ref[at, at] = eye - (a[:, r * NB :] - eye) * lower

    def step(fine):
        for r in range(nb):
            at, end = pl.ds(r * NB, NB), (r + 1) * NB
            hi, lo = halves(x_ref[at, :end])
            yh_ref[at, :end] = hi
            if fine:
                yl_ref[at, :end] = lo
        total = jnp.zeros((1, 1), F32)
        for r in range(nb):
            at, start, end = pl.ds(r * NB, NB), r * NB, (r + 1) * NB
            yh = yh_ref[at, :end]
            t = fast_dot(yh, ah_ref[:end, :end], ((1,), (0,)))
            if fine:
                t += fast_dot(yh, al_ref[:end, :end], ((1,), (0,))) + fast_dot(yl_ref[at, :end], ah_ref[:end, :end], ((1,), (0,)))
            hi, lo = halves(t)
            e = fast_dot(hi, yh_ref[:end, :end], ((1,), (1,)))
            if fine:
                e += fast_dot(lo, yh_ref[:end, :end], ((1,), (1,))) + fast_dot(hi, yl_ref[:end, :end], ((1,), (1,)))
            corner = (e[:, start:] - eye) * lower
            total += jnp.sum(corner * corner, keepdims=True)
            e_ref[at, start:end] = corner.astype(BF)
            if r:
                left = e[:, :start]
                total += jnp.sum(left * left, keepdims=True)
                e_ref[at, :start] = left.astype(BF)
        for r in reversed(range(nb)):
            at, end = pl.ds(r * NB, NB), (r + 1) * NB
            x_ref[at, :end] -= fast_dot(e_ref[at, :end], yh_ref[:end, :end], ((1,), (0,)))
        return total[0, 0]

    def more(tol, most):
        return lambda state: jnp.logical_and(state[0] < most, state[1] > tol)

    _, size = lax.while_loop(more(0.05, 10), lambda s: (s[0] + 1, step(False)), (0, jnp.float32(1e9)))
    _, size = lax.while_loop(more(1e-5, 6), lambda s: (s[0] + 1, step(True)), (0, jnp.float32(1e9)))
    good = size <= 1e-5

    @pl.when(good)
    def _():
        for r in range(nb):
            at, end = pl.ds(r * NB, NB), (r + 1) * NB
            x_ref[at, :end] *= d_ref[:, :end]

    @pl.when(jnp.logical_not(good))
    def _():
        eliminate(a_ref, x_ref, w_ref, s_ref, b_ref)


def chol_inv(a):
    n = a.shape[0]
    square = lambda kind: pltpu.VMEM((n, n), kind)
    return pl.pallas_call(
        chol_kernel,
        out_shape=jax.ShapeDtypeStruct((n, n), F32),
        in_specs=[pl.BlockSpec(memory_space=pltpu.VMEM)],
        out_specs=pl.BlockSpec(memory_space=pltpu.VMEM),
        scratch_shapes=[pltpu.VMEM((NB, NB), F32), square(F32), square(F32), square(BF), square(BF), square(BF), square(BF), square(BF), pltpu.VMEM((1, n), F32)],
        cost_estimate=pl.CostEstimate(flops=10**9, bytes_accessed=2 * 2**20, transcendentals=0),
        compiler_params=pltpu.CompilerParams(vmem_limit_bytes=32 * 2**20),
    )(a)


def mm(a, b, ca, cb):
    return lax.dot_general(a, b, (((ca,), (cb,)), ((), ())), preferred_element_type=F32)


def mm_split(a, b, ca, cb):
    hi = b.astype(BF)
    lo = (b - hi.astype(F32)).astype(BF)
    return mm(a, hi, ca, cb) + mm(a, lo, ca, cb)


def mm_high(a, b, ca, cb):
    return lax.dot_general(a, b, (((ca,), (cb,)), ((), ())), precision=lax.Precision.HIGH, preferred_element_type=F32)


def scatter_sum(x, axis, n):
    parts = lax.all_to_all(x.astype(BF).reshape(n, x.shape[0] // n, x.shape[1]), axis, 0, 0, tiled=True)
    return jnp.sum(parts.astype(F32), axis=0)


def gather(x, axis, n):
    parts = lax.all_to_all(jnp.broadcast_to(x[None], (n,) + x.shape), axis, 0, 0, tiled=True)
    return parts.reshape(n * x.shape[0], x.shape[1])


def row_major(x):
    return with_layout_constraint(x, Layout(tuple(range(x.ndim))))


def tiles(x):
    n, rows, cols = x.shape
    return x.reshape(n, rows // 8, 8, cols // 128, 128).transpose(0, 1, 3, 2, 4).reshape(n, -1, 128)


def finish_kernel(scale, parts_ref, high_ref, low_ref, one_ref, two_ref, out_ref, back_ref):
    nf, rows, rank = parts_ref.shape
    share = rank // nf
    raw = parts_ref[0].astype(F32)
    for g in range(1, nf):
        raw += parts_ref[g].astype(F32)
    hi, lo = halves(raw)
    dims = ((1,), (1,))
    reduced = (fast_dot(hi, high_ref[...], dims) + fast_dot(lo, high_ref[...], dims) + fast_dot(hi, low_ref[...], dims)) * scale
    one = BETA_ONE * one_ref[...] + (1.0 - BETA_ONE) * reduced
    two = BETA_TWO * two_ref[...] + (1.0 - BETA_TWO) * reduced * reduced
    direction = (one / (jnp.sqrt(two) + ADAM_EPS)).astype(BF)
    pad = jnp.zeros((back_ref.shape[2] - rows, rank), F32)
    one = jnp.concatenate([one, pad], axis=0).T
    two = jnp.concatenate([two, pad], axis=0).T
    for g in range(nf):
        out_ref[g] = direction
        at = slice(g * share, (g + 1) * share)
        back_ref[g, :share, :] = one[at].astype(BF)
        back_ref[g, share:, :] = two[at].astype(BF)


def finish(scale, parts, high, low, one, two):
    nf, rows, rank = parts.shape
    back = (nf, 2 * rank // nf, rows + -rows % 128)
    return pl.pallas_call(
        functools.partial(finish_kernel, scale),
        out_shape=[jax.ShapeDtypeStruct(parts.shape, BF), jax.ShapeDtypeStruct(back, BF)],
        in_specs=[pl.BlockSpec(memory_space=pltpu.VMEM)] * 5,
        out_specs=[pl.BlockSpec(memory_space=pltpu.VMEM)] * 2,
        cost_estimate=pl.CostEstimate(flops=10**9, bytes_accessed=6 * 2**20, transcendentals=0),
        compiler_params=pltpu.CompilerParams(vmem_limit_bytes=32 * 2**20),
    )(parts, high, low, one, two)


def unpack_kernel(width, got_ref, one_ref, two_ref):
    share = one_ref.shape[0]
    for ref, first in ((one_ref, 0), (two_ref, share)):
        rows = [got_ref[g, first : first + share, :].astype(F32)[:, :width] for g in range(got_ref.shape[0])]
        ref[...] = jnp.concatenate(rows, axis=1)


def unpack(got, width):
    nf, share, _ = got.shape
    shape = jax.ShapeDtypeStruct((share // 2, nf * width), F32)
    return pl.pallas_call(
        functools.partial(unpack_kernel, width),
        out_shape=[shape, shape],
        in_specs=[pl.BlockSpec(memory_space=pltpu.VMEM)],
        out_specs=[pl.BlockSpec(memory_space=pltpu.VMEM)] * 2,
        cost_estimate=pl.CostEstimate(flops=10**6, bytes_accessed=2**20, transcendentals=0),
    )(got)


def per_device(nf, nt, grad, start_basis, weight, first_moment, second_moment):
    inv_sqrt = 1.0 / math.sqrt(M)
    share_rows, cols = first_moment.shape
    share_cols = cols // nf
    rank = start_basis.shape[1]

    sent = jnp.concatenate([first_moment.astype(BF), second_moment.astype(BF)], axis=0)
    sent = sent.reshape(2 * share_rows, nf, share_cols).transpose(1, 0, 2)
    sent = row_major(jnp.pad(sent, ((0, 0), (0, 0), (0, -share_cols % 128))))

    panel = (scatter_sum(mm(grad, start_basis, 0, 0), "fsdp", nf) * inv_sqrt).astype(BF)
    panel = gather(panel, "fsdp", nf)
    image = scatter_sum(mm(grad, panel, 1, 0), "tp", nt).astype(BF)
    image = lax.all_gather(image, "tp", axis=0, tiled=True)
    raw = scatter_sum(row_major(mm(grad, image, 0, 0).astype(BF)), "fsdp", nf).astype(BF)

    raw = gather(raw, "fsdp", nf)
    rows = rank // nt
    few = rank // nf // nt
    mine = lax.dynamic_slice_in_dim(mm(panel, raw, 0, 0), lax.axis_index("fsdp") * (rank // nf), rank // nf, 0)
    mine = jnp.pad(mine.astype(BF).reshape(nt, few, rank), ((0, 0), (0, -few % 8), (0, 0)))
    both = jnp.concatenate([mm(grad, raw, 1, 0).astype(BF).reshape(nt, rows, rank), mine], axis=1)
    both = jnp.sum(lax.all_to_all(both, "tp", 0, 0, tiled=True).astype(F32), axis=0).astype(BF)
    both = lax.all_gather(both, "tp", axis=0, tiled=False)
    wide = both[:, :rows].reshape(-1, rank)
    gram = both[:, rows : rows + few].reshape(1, rank // nf, rank)
    outer = (mm(wide, wide, 0, 0) / M).astype(BF).reshape(nf, -1, rank)
    raw = row_major(mm(grad, wide, 0, 0).astype(BF))
    got = jnp.concatenate([sent, tiles(outer)], axis=1)
    got = lax.all_to_all(got, "fsdp", 0, 0, tiled=True)
    first_old = got[:, :share_rows].reshape(rank, -1)
    second_old = got[:, share_rows : 2 * share_rows].reshape(rank, -1)
    sums = jnp.sum(got[:, 2 * share_rows :].astype(F32), axis=0).astype(BF)
    grams = gather(jnp.concatenate([sums, tiles(gram)[0]], axis=0), "fsdp", nf)
    grams, raw = lax.optimization_barrier((grams, raw))
    grams = grams.reshape(nf, 2, -1, rank // 128, 8, 128).transpose(1, 0, 2, 4, 3, 5).reshape(2, rank, rank)
    outer, gram = grams[0].astype(F32), grams[1].astype(F32) / M
    inverse = chol_inv(gram)
    second = chol_inv(mm_high(mm_high(inverse, outer, 1, 0), inverse, 1, 1) / M)
    both = mm_high(second, inverse, 1, 0)
    margin = mm_high(gram, both, 0, 1)
    first_basis = mm_split(image, inverse, 1, 1).astype(BF)
    new_basis = (mm_split(wide, both, 1, 1) * inv_sqrt).astype(BF)
    rotated_one = mm(first_old, margin.astype(BF), 0, 0)[:share_cols]
    rotated_two = mm(second_old, (margin * margin).astype(BF), 0, 0)[:share_cols]
    parts = lax.all_to_all(raw.reshape(nf, share_cols, rank), "fsdp", 0, 0, tiled=True)
    rotated_one, rotated_two, first_basis, new_basis = lax.optimization_barrier(
        (rotated_one, rotated_two, first_basis, new_basis)
    )
    direction, back = finish(1.0 / M, parts, *halves(both), rotated_one, rotated_two)
    direction = lax.all_to_all(direction, "fsdp", 0, 0, tiled=True).reshape(cols, rank)
    direction, back = lax.optimization_barrier((direction, back))
    moment_one, moment_two = unpack(lax.all_to_all(back, "fsdp", 0, 0, tiled=True), share_cols)
    expanded = mm(new_basis, direction, 1, 1)
    new_weight = (weight.astype(F32) - STEP_SIZE * inv_sqrt * expanded).astype(BF)
    return (first_basis, new_basis, moment_one, moment_two, new_weight)


def solution(mesh):
    specs = (P("fsdp", "tp"), P("fsdp", None), P("fsdp", "tp"), P("fsdp", "tp"), P("fsdp", "tp"))
    out_specs = (P("fsdp", None), P("fsdp", None), P("fsdp", "tp"), P("fsdp", "tp"), P("fsdp", "tp"))
    nf, nt = mesh.shape["fsdp"], mesh.shape["tp"]

    def body(*args):
        return per_device(nf, nt, *args)

    return jax.shard_map(body, mesh=mesh, in_specs=specs, out_specs=out_specs, check_vma=False)
```

```python
import functools
import math

import jax
import jax.numpy as jnp
from jax import lax
from jax.experimental import pallas as pl
from jax.experimental.pallas import tpu as pltpu
from jax.experimental.layout import Layout, with_layout_constraint
from jax.sharding import PartitionSpec as P

M = 8192

BETA_ONE = 0.9
BETA_TWO = 0.95
ADAM_EPS = 1e-06
STEP_SIZE = 2.0

BF = jnp.bfloat16
F32 = jnp.float32

def elim(read, n=128):
    lane = lax.broadcasted_iota(jnp.int32, (8, n), 1)
    sub = lax.broadcasted_iota(jnp.int32, (8, n), 0)
    G = [read(g) for g in range(n // 8)]
    out = []
    for g0 in range(n // 8):
        acc = jnp.zeros((8, n), jnp.float32)
        for s0 in range(8):
            j = g0 * 8 + s0
            hit = lane == j
            r = jnp.broadcast_to(G[g0][s0:s0 + 1, :], (8, n))
            p = jnp.broadcast_to(r[:, j:j + 1], (8, n))
            row = jnp.where(lane < j, r, jnp.where(hit, 1.0, 0.0)) * lax.rsqrt(p)
            acc = jnp.where(sub == s0, row, acc)
            rr = jnp.where(hit, 1.0, r) * (1.0 / p)
            for g in range(g0, n // 8):
                c = jnp.broadcast_to(G[g][:, j:j + 1], (8, n))
                new = jnp.where(hit, 0.0, G[g]) - c * rr
                G[g] = jnp.where(sub > s0, new, G[g]) if g == g0 else new
        out.append(acc)
    return out


NB = 128


def exact_dot(a, b, dims):
    return lax.dot_general(a, b, (dims, ((), ())), precision=lax.Precision.HIGHEST, preferred_element_type=F32)


def fast_dot(a, b, dims):
    return lax.dot_general(a, b, (dims, ((), ())), preferred_element_type=F32)


def halves(x):
    hi = x.astype(BF)
    return hi, (x - hi.astype(F32)).astype(BF)


def eliminate(a_ref, x_ref, w_ref, s_ref, b_ref):
    n = a_ref.shape[0]
    nb = n // NB
    s_ref[...] = a_ref[...]
    b_ref[...] = jnp.zeros_like(b_ref)
    x_ref[...] = jnp.zeros_like(x_ref)

    @pl.loop(0, nb)
    def _(k):
        rows = pl.ds(pl.multiple_of(k * NB, NB), NB)
        for g, v in enumerate(elim(lambda g: s_ref[pl.ds(pl.multiple_of(k * NB + 8 * g, 8), 8), rows])):
            w_ref[pl.ds(8 * g, 8), :] = v
        w = w_ref[...]
        u = exact_dot(w, s_ref[rows, :], ((1,), (0,)))
        x_ref[rows, :] = exact_dot(w, b_ref[rows, :], ((1,), (0,)))
        x_ref[rows, rows] = w

        @pl.loop(k + 1, nb)
        def _(i):
            below = pl.ds(pl.multiple_of(i * NB, NB), NB)
            ui = exact_dot(w, s_ref[rows, below], ((1,), (0,)))
            s_ref[below, :] -= exact_dot(ui, u, ((0,), (0,)))
            b_ref[below, :] -= exact_dot(ui, x_ref[rows, :], ((0,), (0,)))


def chol_kernel(a_ref, x_ref, w_ref, s_ref, b_ref, ah_ref, al_ref, yh_ref, yl_ref, e_ref, d_ref):
    n = a_ref.shape[0]
    nb = n // NB
    eye = (lax.broadcasted_iota(jnp.int32, (NB, NB), 0) == lax.broadcasted_iota(jnp.int32, (NB, NB), 1)).astype(F32)
    lower = (lax.broadcasted_iota(jnp.int32, (NB, NB), 0) > lax.broadcasted_iota(jnp.int32, (NB, NB), 1)).astype(F32) + 0.5 * eye

    for r in range(nb):
        at = pl.ds(r * NB, NB)
        d_ref[:, at] = lax.rsqrt(jnp.sum(a_ref[at, at] * eye, axis=0, keepdims=True))
    for r in range(nb):
        at = pl.ds(r * NB, NB)
        here = jnp.sum(eye * d_ref[:, at], axis=1, keepdims=True)
        hi, lo = halves(a_ref[at, :] * here * d_ref[...])
        ah_ref[at, :] = hi
        al_ref[at, :] = lo
    x_ref[...] = jnp.zeros_like(x_ref)
    yh_ref[...] = jnp.zeros_like(yh_ref)
    yl_ref[...] = jnp.zeros_like(yl_ref)
    for r in range(nb):
        at = pl.ds(r * NB, NB)
        end = (r + 1) * NB
        a = ah_ref[at, :end].astype(F32)
        if r:
            x_ref[at, : r * NB] = -a[:, : r * NB]
        x_ref[at, at] = eye - (a[:, r * NB :] - eye) * lower

    def step(fine):
        for r in range(nb):
            at, end = pl.ds(r * NB, NB), (r + 1) * NB
            hi, lo = halves(x_ref[at, :end])
            yh_ref[at, :end] = hi
            if fine:
                yl_ref[at, :end] = lo
        total = jnp.zeros((1, 1), F32)
        for r in range(nb):
            at, start, end = pl.ds(r * NB, NB), r * NB, (r + 1) * NB
            yh = yh_ref[at, :end]
            t = fast_dot(yh, ah_ref[:end, :end], ((1,), (0,)))
            if fine:
                t += fast_dot(yh, al_ref[:end, :end], ((1,), (0,))) + fast_dot(yl_ref[at, :end], ah_ref[:end, :end], ((1,), (0,)))
            hi, lo = halves(t)
            e = fast_dot(hi, yh_ref[:end, :end], ((1,), (1,)))
            if fine:
                e += fast_dot(lo, yh_ref[:end, :end], ((1,), (1,))) + fast_dot(hi, yl_ref[:end, :end], ((1,), (1,)))
            corner = (e[:, start:] - eye) * lower
            total += jnp.sum(corner * corner, keepdims=True)
            e_ref[at, start:end] = corner.astype(BF)
            if r:
                left = e[:, :start]
                total += jnp.sum(left * left, keepdims=True)
                e_ref[at, :start] = left.astype(BF)
        for r in reversed(range(nb)):
            at, end = pl.ds(r * NB, NB), (r + 1) * NB
            x_ref[at, :end] -= fast_dot(e_ref[at, :end], yh_ref[:end, :end], ((1,), (0,)))
        return total[0, 0]

    def more(tol, most):
        return lambda state: jnp.logical_and(state[0] < most, state[1] > tol)

    _, size = lax.while_loop(more(0.05, 10), lambda s: (s[0] + 1, step(False)), (0, jnp.float32(1e9)))
    _, size = lax.while_loop(more(1e-5, 6), lambda s: (s[0] + 1, step(True)), (0, jnp.float32(1e9)))
    good = size <= 1e-5

    @pl.when(good)
    def _():
        for r in range(nb):
            at, end = pl.ds(r * NB, NB), (r + 1) * NB
            x_ref[at, :end] *= d_ref[:, :end]

    @pl.when(jnp.logical_not(good))
    def _():
        eliminate(a_ref, x_ref, w_ref, s_ref, b_ref)


def chol_inv(a):
    n = a.shape[0]
    square = lambda kind: pltpu.VMEM((n, n), kind)
    return pl.pallas_call(
        chol_kernel,
        out_shape=jax.ShapeDtypeStruct((n, n), F32),
        in_specs=[pl.BlockSpec(memory_space=pltpu.VMEM)],
        out_specs=pl.BlockSpec(memory_space=pltpu.VMEM),
        scratch_shapes=[pltpu.VMEM((NB, NB), F32), square(F32), square(F32), square(BF), square(BF), square(BF), square(BF), square(BF), pltpu.VMEM((1, n), F32)],
        cost_estimate=pl.CostEstimate(flops=10**9, bytes_accessed=2 * 2**20, transcendentals=0),
        compiler_params=pltpu.CompilerParams(vmem_limit_bytes=32 * 2**20),
    )(a)


def mm(a, b, ca, cb):
    return lax.dot_general(a, b, (((ca,), (cb,)), ((), ())), preferred_element_type=F32)


def mm_split(a, b, ca, cb):
    hi = b.astype(BF)
    lo = (b - hi.astype(F32)).astype(BF)
    return mm(a, hi, ca, cb) + mm(a, lo, ca, cb)


def mm_high(a, b, ca, cb):
    return lax.dot_general(a, b, (((ca,), (cb,)), ((), ())), precision=lax.Precision.HIGH, preferred_element_type=F32)


def scatter_sum(x, axis, n):
    parts = lax.all_to_all(x.astype(BF).reshape(n, x.shape[0] // n, x.shape[1]), axis, 0, 0, tiled=True)
    return jnp.sum(parts.astype(F32), axis=0)


def gather(x, axis, n):
    parts = lax.all_to_all(jnp.broadcast_to(x[None], (n,) + x.shape), axis, 0, 0, tiled=True)
    return parts.reshape(n * x.shape[0], x.shape[1])


def row_major(x):
    return with_layout_constraint(x, Layout(tuple(range(x.ndim))))


def tiles(x):
    n, rows, cols = x.shape
    return x.reshape(n, rows // 8, 8, cols // 128, 128).transpose(0, 1, 3, 2, 4).reshape(n, -1, 128)


def finish_kernel(scale, parts_ref, high_ref, low_ref, one_ref, two_ref, out_ref, back_ref):
    nf, rows, rank = parts_ref.shape
    share = rank // nf
    raw = parts_ref[0].astype(F32)
    for g in range(1, nf):
        raw += parts_ref[g].astype(F32)
    hi, lo = halves(raw)
    dims = ((1,), (1,))
    reduced = (fast_dot(hi, high_ref[...], dims) + fast_dot(lo, high_ref[...], dims) + fast_dot(hi, low_ref[...], dims)) * scale
    one = BETA_ONE * one_ref[...] + (1.0 - BETA_ONE) * reduced
    two = BETA_TWO * two_ref[...] + (1.0 - BETA_TWO) * reduced * reduced
    direction = (one / (jnp.sqrt(two) + ADAM_EPS)).astype(BF)
    pad = jnp.zeros((back_ref.shape[2] - rows, rank), F32)
    one = jnp.concatenate([one, pad], axis=0).T
    two = jnp.concatenate([two, pad], axis=0).T
    for g in range(nf):
        out_ref[g] = direction
        at = slice(g * share, (g + 1) * share)
        back_ref[g, :share, :] = one[at].astype(BF)
        back_ref[g, share:, :] = two[at].astype(BF)


def finish(scale, parts, high, low, one, two):
    nf, rows, rank = parts.shape
    back = (nf, 2 * rank // nf, rows + -rows % 128)
    return pl.pallas_call(
        functools.partial(finish_kernel, scale),
        out_shape=[jax.ShapeDtypeStruct(parts.shape, BF), jax.ShapeDtypeStruct(back, BF)],
        in_specs=[pl.BlockSpec(memory_space=pltpu.VMEM)] * 5,
        out_specs=[pl.BlockSpec(memory_space=pltpu.VMEM)] * 2,
        cost_estimate=pl.CostEstimate(flops=10**9, bytes_accessed=6 * 2**20, transcendentals=0),
        compiler_params=pltpu.CompilerParams(vmem_limit_bytes=32 * 2**20),
    )(parts, high, low, one, two)


def unpack_kernel(width, got_ref, one_ref, two_ref):
    share = one_ref.shape[0]
    for ref, first in ((one_ref, 0), (two_ref, share)):
        rows = [got_ref[g, first : first + share, :].astype(F32)[:, :width] for g in range(got_ref.shape[0])]
        ref[...] = jnp.concatenate(rows, axis=1)


def unpack(got, width):
    nf, share, _ = got.shape
    shape = jax.ShapeDtypeStruct((share // 2, nf * width), F32)
    return pl.pallas_call(
        functools.partial(unpack_kernel, width),
        out_shape=[shape, shape],
        in_specs=[pl.BlockSpec(memory_space=pltpu.VMEM)],
        out_specs=[pl.BlockSpec(memory_space=pltpu.VMEM)] * 2,
        cost_estimate=pl.CostEstimate(flops=10**6, bytes_accessed=2**20, transcendentals=0),
    )(got)


def per_device(nf, nt, grad, start_basis, weight, first_moment, second_moment):
    inv_sqrt = 1.0 / math.sqrt(M)
    share_rows, cols = first_moment.shape
    share_cols = cols // nf
    rank = start_basis.shape[1]

    sent = jnp.concatenate([first_moment.astype(BF), second_moment.astype(BF)], axis=0)
    sent = sent.reshape(2 * share_rows, nf, share_cols).transpose(1, 0, 2)
    sent = row_major(jnp.pad(sent, ((0, 0), (0, 0), (0, -share_cols % 128))))

    panel = (scatter_sum(mm(grad, start_basis, 0, 0), "fsdp", nf) * inv_sqrt).astype(BF)
    panel = gather(panel, "fsdp", nf)
    image = scatter_sum(mm(grad, panel, 1, 0), "tp", nt).astype(BF)
    image, sent = lax.optimization_barrier((image, sent))
    image = lax.all_gather(image, "tp", axis=0, tiled=True)
    got = lax.all_to_all(sent, "fsdp", 0, 0, tiled=True)
    image, got = lax.optimization_barrier((image, got))
    first_old = got[:, :share_rows].reshape(rank, -1)
    second_old = got[:, share_rows:].reshape(rank, -1)
    raw = scatter_sum(row_major(mm(grad, image, 0, 0).astype(BF)), "fsdp", nf).astype(BF)

    raw = gather(raw, "fsdp", nf)
    rows = rank // nt
    few = rank // nf // nt
    mine = lax.dynamic_slice_in_dim(mm(panel, raw, 0, 0), lax.axis_index("fsdp") * (rank // nf), rank // nf, 0)
    mine = jnp.pad(mine.astype(BF).reshape(nt, few, rank), ((0, 0), (0, -few % 8), (0, 0)))
    both = jnp.concatenate([mm(grad, raw, 1, 0).astype(BF).reshape(nt, rows, rank), mine], axis=1)
    both = jnp.sum(lax.all_to_all(both, "tp", 0, 0, tiled=True).astype(F32), axis=0).astype(BF)
    outer = (mm(both[:rows], both[:rows], 0, 0) / M).astype(BF).reshape(nf, -1, rank)
    outer = lax.all_to_all(tiles(outer), "fsdp", 0, 0, tiled=True)
    both = lax.all_gather(both, "tp", axis=0, tiled=False)
    wide = both[:, :rows].reshape(-1, rank)
    gram = both[:, rows : rows + few].reshape(1, rank // nf, rank)
    raw = row_major(mm(grad, wide, 0, 0).astype(BF))
    sums = jnp.sum(outer.astype(F32), axis=0).astype(BF)
    sums = jnp.sum(lax.all_gather(sums, "tp", axis=0, tiled=False).astype(F32), axis=0).astype(BF)
    grams = gather(jnp.concatenate([sums, tiles(gram)[0]], axis=0), "fsdp", nf)
    grams, raw = lax.optimization_barrier((grams, raw))
    grams = grams.reshape(nf, 2, -1, rank // 128, 8, 128).transpose(1, 0, 2, 4, 3, 5).reshape(2, rank, rank)
    outer, gram = grams[0].astype(F32), grams[1].astype(F32) / M
    inverse = chol_inv(gram)
    second = chol_inv(mm_high(mm_high(inverse, outer, 1, 0), inverse, 1, 1) / M)
    both = mm_high(second, inverse, 1, 0)
    margin = mm_high(gram, both, 0, 1)
    first_basis = mm_split(image, inverse, 1, 1).astype(BF)
    new_basis = (mm_split(wide, both, 1, 1) * inv_sqrt).astype(BF)
    rotated_one = mm(first_old, margin.astype(BF), 0, 0)[:share_cols]
    rotated_two = mm(second_old, (margin * margin).astype(BF), 0, 0)[:share_cols]
    parts = lax.all_to_all(raw.reshape(nf, share_cols, rank), "fsdp", 0, 0, tiled=True)
    rotated_one, rotated_two, first_basis, new_basis = lax.optimization_barrier(
        (rotated_one, rotated_two, first_basis, new_basis)
    )
    direction, back = finish(1.0 / M, parts, *halves(both), rotated_one, rotated_two)
    direction = lax.all_to_all(direction, "fsdp", 0, 0, tiled=True).reshape(cols, rank)
    direction, back = lax.optimization_barrier((direction, back))
    moment_one, moment_two = unpack(lax.all_to_all(back, "fsdp", 0, 0, tiled=True), share_cols)
    expanded = mm(new_basis, direction, 1, 1)
    new_weight = (weight.astype(F32) - STEP_SIZE * inv_sqrt * expanded).astype(BF)
    return (first_basis, new_basis, moment_one, moment_two, new_weight)


def solution(mesh):
    specs = (P("fsdp", "tp"), P("fsdp", None), P("fsdp", "tp"), P("fsdp", "tp"), P("fsdp", "tp"))
    out_specs = (P("fsdp", None), P("fsdp", None), P("fsdp", "tp"), P("fsdp", "tp"), P("fsdp", "tp"))
    nf, nt = mesh.shape["fsdp"], mesh.shape["tp"]

    def body(*args):
        return per_device(nf, nt, *args)

    return jax.shard_map(body, mesh=mesh, in_specs=specs, out_specs=out_specs, check_vma=False)
```

```python
import functools
import math

import jax
import jax.numpy as jnp
from jax import lax
from jax.experimental import pallas as pl
from jax.experimental.pallas import tpu as pltpu
from jax.experimental.layout import Layout, with_layout_constraint
from jax.sharding import PartitionSpec as P

M = 8192

BETA_ONE = 0.9
BETA_TWO = 0.95
ADAM_EPS = 1e-06
STEP_SIZE = 2.0

BF = jnp.bfloat16
F32 = jnp.float32

def elim(read, n=128):
    lane = lax.broadcasted_iota(jnp.int32, (8, n), 1)
    sub = lax.broadcasted_iota(jnp.int32, (8, n), 0)
    G = [read(g) for g in range(n // 8)]
    out = []
    for g0 in range(n // 8):
        acc = jnp.zeros((8, n), jnp.float32)
        for s0 in range(8):
            j = g0 * 8 + s0
            hit = lane == j
            r = jnp.broadcast_to(G[g0][s0:s0 + 1, :], (8, n))
            p = jnp.broadcast_to(r[:, j:j + 1], (8, n))
            row = jnp.where(lane < j, r, jnp.where(hit, 1.0, 0.0)) * lax.rsqrt(p)
            acc = jnp.where(sub == s0, row, acc)
            rr = jnp.where(hit, 1.0, r) * (1.0 / p)
            for g in range(g0, n // 8):
                c = jnp.broadcast_to(G[g][:, j:j + 1], (8, n))
                new = jnp.where(hit, 0.0, G[g]) - c * rr
                G[g] = jnp.where(sub > s0, new, G[g]) if g == g0 else new
        out.append(acc)
    return out


NB = 128


def exact_dot(a, b, dims):
    return lax.dot_general(a, b, (dims, ((), ())), precision=lax.Precision.HIGHEST, preferred_element_type=F32)


def fast_dot(a, b, dims):
    return lax.dot_general(a, b, (dims, ((), ())), preferred_element_type=F32)


def halves(x):
    hi = x.astype(BF)
    return hi, (x - hi.astype(F32)).astype(BF)


def eliminate(a_ref, x_ref, w_ref, s_ref, b_ref):
    n = a_ref.shape[0]
    nb = n // NB
    s_ref[...] = a_ref[...]
    b_ref[...] = jnp.zeros_like(b_ref)
    x_ref[...] = jnp.zeros_like(x_ref)

    @pl.loop(0, nb)
    def _(k):
        rows = pl.ds(pl.multiple_of(k * NB, NB), NB)
        for g, v in enumerate(elim(lambda g: s_ref[pl.ds(pl.multiple_of(k * NB + 8 * g, 8), 8), rows])):
            w_ref[pl.ds(8 * g, 8), :] = v
        w = w_ref[...]
        u = exact_dot(w, s_ref[rows, :], ((1,), (0,)))
        x_ref[rows, :] = exact_dot(w, b_ref[rows, :], ((1,), (0,)))
        x_ref[rows, rows] = w

        @pl.loop(k + 1, nb)
        def _(i):
            below = pl.ds(pl.multiple_of(i * NB, NB), NB)
            ui = exact_dot(w, s_ref[rows, below], ((1,), (0,)))
            s_ref[below, :] -= exact_dot(ui, u, ((0,), (0,)))
            b_ref[below, :] -= exact_dot(ui, x_ref[rows, :], ((0,), (0,)))


def chol_kernel(a_ref, x_ref, w_ref, s_ref, b_ref, ah_ref, al_ref, yh_ref, yl_ref, e_ref, d_ref):
    n = a_ref.shape[0]
    nb = n // NB
    eye = (lax.broadcasted_iota(jnp.int32, (NB, NB), 0) == lax.broadcasted_iota(jnp.int32, (NB, NB), 1)).astype(F32)
    lower = (lax.broadcasted_iota(jnp.int32, (NB, NB), 0) > lax.broadcasted_iota(jnp.int32, (NB, NB), 1)).astype(F32) + 0.5 * eye

    for r in range(nb):
        at = pl.ds(r * NB, NB)
        d_ref[:, at] = lax.rsqrt(jnp.sum(a_ref[at, at] * eye, axis=0, keepdims=True))
    for r in range(nb):
        at = pl.ds(r * NB, NB)
        here = jnp.sum(eye * d_ref[:, at], axis=1, keepdims=True)
        hi, lo = halves(a_ref[at, :] * here * d_ref[...])
        ah_ref[at, :] = hi
        al_ref[at, :] = lo
    x_ref[...] = jnp.zeros_like(x_ref)
    yh_ref[...] = jnp.zeros_like(yh_ref)
    yl_ref[...] = jnp.zeros_like(yl_ref)
    for r in range(nb):
        at = pl.ds(r * NB, NB)
        end = (r + 1) * NB
        a = ah_ref[at, :end].astype(F32)
        if r:
            x_ref[at, : r * NB] = -a[:, : r * NB]
        x_ref[at, at] = eye - (a[:, r * NB :] - eye) * lower

    def step(fine):
        for r in range(nb):
            at, end = pl.ds(r * NB, NB), (r + 1) * NB
            hi, lo = halves(x_ref[at, :end])
            yh_ref[at, :end] = hi
            if fine:
                yl_ref[at, :end] = lo
        total = jnp.zeros((1, 1), F32)
        for r in range(nb):
            at, start, end = pl.ds(r * NB, NB), r * NB, (r + 1) * NB
            yh = yh_ref[at, :end]
            t = fast_dot(yh, ah_ref[:end, :end], ((1,), (0,)))
            if fine:
                t += fast_dot(yh, al_ref[:end, :end], ((1,), (0,))) + fast_dot(yl_ref[at, :end], ah_ref[:end, :end], ((1,), (0,)))
            hi, lo = halves(t)
            e = fast_dot(hi, yh_ref[:end, :end], ((1,), (1,)))
            if fine:
                e += fast_dot(lo, yh_ref[:end, :end], ((1,), (1,))) + fast_dot(hi, yl_ref[:end, :end], ((1,), (1,)))
            corner = (e[:, start:] - eye) * lower
            total += jnp.sum(corner * corner, keepdims=True)
            e_ref[at, start:end] = corner.astype(BF)
            if r:
                left = e[:, :start]
                total += jnp.sum(left * left, keepdims=True)
                e_ref[at, :start] = left.astype(BF)
        for r in reversed(range(nb)):
            at, end = pl.ds(r * NB, NB), (r + 1) * NB
            x_ref[at, :end] -= fast_dot(e_ref[at, :end], yh_ref[:end, :end], ((1,), (0,)))
        return total[0, 0]

    def more(tol, most):
        return lambda state: jnp.logical_and(state[0] < most, state[1] > tol)

    _, size = lax.while_loop(more(0.05, 10), lambda s: (s[0] + 1, step(False)), (0, jnp.float32(1e9)))
    _, size = lax.while_loop(more(1e-5, 6), lambda s: (s[0] + 1, step(True)), (0, jnp.float32(1e9)))
    good = size <= 1e-5

    @pl.when(good)
    def _():
        for r in range(nb):
            at, end = pl.ds(r * NB, NB), (r + 1) * NB
            x_ref[at, :end] *= d_ref[:, :end]

    @pl.when(jnp.logical_not(good))
    def _():
        eliminate(a_ref, x_ref, w_ref, s_ref, b_ref)


def chol_inv(a):
    n = a.shape[0]
    square = lambda kind: pltpu.VMEM((n, n), kind)
    return pl.pallas_call(
        chol_kernel,
        out_shape=jax.ShapeDtypeStruct((n, n), F32),
        in_specs=[pl.BlockSpec(memory_space=pltpu.VMEM)],
        out_specs=pl.BlockSpec(memory_space=pltpu.VMEM),
        scratch_shapes=[pltpu.VMEM((NB, NB), F32), square(F32), square(F32), square(BF), square(BF), square(BF), square(BF), square(BF), pltpu.VMEM((1, n), F32)],
        cost_estimate=pl.CostEstimate(flops=10**6, bytes_accessed=2**10, transcendentals=0),
        compiler_params=pltpu.CompilerParams(vmem_limit_bytes=32 * 2**20),
    )(a)


def mm(a, b, ca, cb):
    return lax.dot_general(a, b, (((ca,), (cb,)), ((), ())), preferred_element_type=F32)


def mm_split(a, b, ca, cb):
    hi = b.astype(BF)
    lo = (b - hi.astype(F32)).astype(BF)
    return mm(a, hi, ca, cb) + mm(a, lo, ca, cb)


def mm_high(a, b, ca, cb):
    return lax.dot_general(a, b, (((ca,), (cb,)), ((), ())), precision=lax.Precision.HIGH, preferred_element_type=F32)


def scatter_sum(x, axis, n):
    parts = lax.all_to_all(x.astype(BF).reshape(n, x.shape[0] // n, x.shape[1]), axis, 0, 0, tiled=True)
    return jnp.sum(parts.astype(F32), axis=0)


def gather(x, axis, n):
    parts = lax.all_to_all(jnp.broadcast_to(x[None], (n,) + x.shape), axis, 0, 0, tiled=True)
    return parts.reshape(n * x.shape[0], x.shape[1])


def row_major(x):
    return with_layout_constraint(x, Layout(tuple(range(x.ndim))))


def tiles(x):
    n, rows, cols = x.shape
    return x.reshape(n, rows // 8, 8, cols // 128, 128).transpose(0, 1, 3, 2, 4).reshape(n, -1, 128)


def finish_kernel(scale, parts_ref, high_ref, low_ref, one_ref, two_ref, out_ref, back_ref):
    nf, rows, rank = parts_ref.shape
    share = rank // nf
    raw = parts_ref[0].astype(F32)
    for g in range(1, nf):
        raw += parts_ref[g].astype(F32)
    hi, lo = halves(raw)
    dims = ((1,), (1,))
    reduced = (fast_dot(hi, high_ref[...], dims) + fast_dot(lo, high_ref[...], dims) + fast_dot(hi, low_ref[...], dims)) * scale
    one = BETA_ONE * one_ref[...] + (1.0 - BETA_ONE) * reduced
    two = BETA_TWO * two_ref[...] + (1.0 - BETA_TWO) * reduced * reduced
    direction = (one / (jnp.sqrt(two) + ADAM_EPS)).astype(BF)
    pad = jnp.zeros((back_ref.shape[2] - rows, rank), F32)
    one = jnp.concatenate([one, pad], axis=0).T
    two = jnp.concatenate([two, pad], axis=0).T
    for g in range(nf):
        out_ref[g] = direction
        at = slice(g * share, (g + 1) * share)
        back_ref[g, :share, :] = one[at].astype(BF)
        back_ref[g, share:, :] = two[at].astype(BF)


def finish(scale, parts, high, low, one, two):
    nf, rows, rank = parts.shape
    back = (nf, 2 * rank // nf, rows + -rows % 128)
    return pl.pallas_call(
        functools.partial(finish_kernel, scale),
        out_shape=[jax.ShapeDtypeStruct(parts.shape, BF), jax.ShapeDtypeStruct(back, BF)],
        in_specs=[pl.BlockSpec(memory_space=pltpu.VMEM)] * 5,
        out_specs=[pl.BlockSpec(memory_space=pltpu.VMEM)] * 2,
        cost_estimate=pl.CostEstimate(flops=10**9, bytes_accessed=6 * 2**20, transcendentals=0),
        compiler_params=pltpu.CompilerParams(vmem_limit_bytes=32 * 2**20),
    )(parts, high, low, one, two)


def unpack_kernel(width, got_ref, one_ref, two_ref):
    share = one_ref.shape[0]
    for ref, first in ((one_ref, 0), (two_ref, share)):
        rows = [got_ref[g, first : first + share, :].astype(F32)[:, :width] for g in range(got_ref.shape[0])]
        ref[...] = jnp.concatenate(rows, axis=1)


def unpack(got, width):
    nf, share, _ = got.shape
    shape = jax.ShapeDtypeStruct((share // 2, nf * width), F32)
    return pl.pallas_call(
        functools.partial(unpack_kernel, width),
        out_shape=[shape, shape],
        in_specs=[pl.BlockSpec(memory_space=pltpu.VMEM)],
        out_specs=[pl.BlockSpec(memory_space=pltpu.VMEM)] * 2,
        cost_estimate=pl.CostEstimate(flops=10**6, bytes_accessed=2**20, transcendentals=0),
    )(got)


def per_device(nf, nt, grad, start_basis, weight, first_moment, second_moment):
    inv_sqrt = 1.0 / math.sqrt(M)
    share_rows, cols = first_moment.shape
    share_cols = cols // nf
    rank = start_basis.shape[1]

    sent = jnp.concatenate([first_moment.astype(BF), second_moment.astype(BF)], axis=0)
    sent = sent.reshape(2 * share_rows, nf, share_cols).transpose(1, 0, 2)
    sent = row_major(jnp.pad(sent, ((0, 0), (0, 0), (0, -share_cols % 128))))

    first_row = (lax.axis_index("fsdp") * (rank // nf)).astype(jnp.uint32)
    panel, first_row = lax.optimization_barrier((mm(grad, start_basis, 0, 0).astype(BF), first_row))
    panel = (scatter_sum(panel, "fsdp", nf) * inv_sqrt).astype(BF)
    panel = gather(panel, "fsdp", nf)
    image = scatter_sum(mm(grad, panel, 1, 0), "tp", nt).astype(BF)
    image = lax.all_gather(image, "tp", axis=0, tiled=True)
    raw = scatter_sum(row_major(mm(grad, image, 0, 0).astype(BF)), "fsdp", nf).astype(BF)

    raw = gather(raw, "fsdp", nf)
    rows = rank // nt
    few = rank // nf // nt
    mine = lax.dynamic_slice(mm(panel, raw, 0, 0), (first_row, jnp.uint32(0)), (rank // nf, rank))
    mine = jnp.pad(mine.astype(BF).reshape(nt, few, rank), ((0, 0), (0, -few % 8), (0, 0)))
    both = jnp.concatenate([mm(grad, raw, 1, 0).astype(BF).reshape(nt, rows, rank), mine], axis=1)
    both = jnp.sum(lax.all_to_all(both, "tp", 0, 0, tiled=True).astype(F32), axis=0).astype(BF)
    both = lax.all_gather(both, "tp", axis=0, tiled=False)
    wide = both[:, :rows].reshape(-1, rank)
    gram = both[:, rows : rows + few].reshape(1, rank // nf, rank)
    outer = (mm(wide, wide, 0, 0) / M).astype(BF).reshape(nf, -1, rank)
    raw = row_major(mm(grad, wide, 0, 0).astype(BF))
    got = jnp.concatenate([sent, tiles(outer)], axis=1)
    got = lax.all_to_all(got, "fsdp", 0, 0, tiled=True)
    first_old = got[:, :share_rows].reshape(rank, -1)
    second_old = got[:, share_rows : 2 * share_rows].reshape(rank, -1)
    sums = jnp.sum(got[:, 2 * share_rows :].astype(F32), axis=0).astype(BF)
    grams = gather(jnp.concatenate([sums, tiles(gram)[0]], axis=0), "fsdp", nf)
    grams, raw = lax.optimization_barrier((grams, raw))
    grams = grams.reshape(nf, 2, -1, rank // 128, 8, 128).transpose(1, 0, 2, 4, 3, 5).reshape(2, rank, rank)
    outer, gram = grams[0].astype(F32), grams[1].astype(F32) / M
    inverse = chol_inv(gram)
    second = chol_inv(mm_high(mm_high(inverse, outer, 1, 0), inverse, 1, 1) / M)
    both = mm_high(second, inverse, 1, 0)
    margin = mm_high(gram, both, 0, 1)
    first_basis = mm_split(image, inverse, 1, 1).astype(BF)
    new_basis = (mm_split(wide, both, 1, 1) * inv_sqrt).astype(BF)
    rotated_one = mm(first_old, margin.astype(BF), 0, 0)[:share_cols]
    rotated_two = mm(second_old, (margin * margin).astype(BF), 0, 0)[:share_cols]
    parts = lax.all_to_all(raw.reshape(nf, share_cols, rank), "fsdp", 0, 0, tiled=True)
    rotated_one, rotated_two, first_basis, new_basis = lax.optimization_barrier(
        (rotated_one, rotated_two, first_basis, new_basis)
    )
    direction, back = finish(1.0 / M, parts, *halves(both), rotated_one, rotated_two)
    direction = lax.all_to_all(direction, "fsdp", 0, 0, tiled=True).reshape(cols, rank)
    direction, back = lax.optimization_barrier((direction, back))
    moment_one, moment_two = unpack(lax.all_to_all(back, "fsdp", 0, 0, tiled=True), share_cols)
    expanded = mm(new_basis, direction, 1, 1)
    new_weight = (weight.astype(F32) - STEP_SIZE * inv_sqrt * expanded).astype(BF)
    return (first_basis, new_basis, moment_one, moment_two, new_weight)


def solution(mesh):
    specs = (P("fsdp", "tp"), P("fsdp", None), P("fsdp", "tp"), P("fsdp", "tp"), P("fsdp", "tp"))
    out_specs = (P("fsdp", None), P("fsdp", None), P("fsdp", "tp"), P("fsdp", "tp"), P("fsdp", "tp"))
    nf, nt = mesh.shape["fsdp"], mesh.shape["tp"]

    def body(*args):
        return per_device(nf, nt, *args)

    return jax.shard_map(body, mesh=mesh, in_specs=specs, out_specs=out_specs, check_vma=False)
```

```python
import functools
import math

import jax
import jax.numpy as jnp
from jax import lax
from jax.experimental import pallas as pl
from jax.experimental.pallas import tpu as pltpu
from jax.experimental.layout import Layout, with_layout_constraint
from jax.sharding import PartitionSpec as P

M = 8192

BETA_ONE = 0.9
BETA_TWO = 0.95
ADAM_EPS = 1e-06
STEP_SIZE = 2.0

BF = jnp.bfloat16
F32 = jnp.float32

def elim(read, n=128):
    lane = lax.broadcasted_iota(jnp.int32, (8, n), 1)
    sub = lax.broadcasted_iota(jnp.int32, (8, n), 0)
    G = [read(g) for g in range(n // 8)]
    out = []
    for g0 in range(n // 8):
        acc = jnp.zeros((8, n), jnp.float32)
        for s0 in range(8):
            j = g0 * 8 + s0
            hit = lane == j
            r = jnp.broadcast_to(G[g0][s0:s0 + 1, :], (8, n))
            p = jnp.broadcast_to(r[:, j:j + 1], (8, n))
            row = jnp.where(lane < j, r, jnp.where(hit, 1.0, 0.0)) * lax.rsqrt(p)
            acc = jnp.where(sub == s0, row, acc)
            rr = jnp.where(hit, 1.0, r) * (1.0 / p)
            for g in range(g0, n // 8):
                c = jnp.broadcast_to(G[g][:, j:j + 1], (8, n))
                new = jnp.where(hit, 0.0, G[g]) - c * rr
                G[g] = jnp.where(sub > s0, new, G[g]) if g == g0 else new
        out.append(acc)
    return out


NB = 128


def exact_dot(a, b, dims):
    return lax.dot_general(a, b, (dims, ((), ())), precision=lax.Precision.HIGHEST, preferred_element_type=F32)


def fast_dot(a, b, dims):
    return lax.dot_general(a, b, (dims, ((), ())), preferred_element_type=F32)


def halves(x):
    hi = x.astype(BF)
    return hi, (x - hi.astype(F32)).astype(BF)


def eliminate(a_ref, x_ref, w_ref, s_ref, b_ref):
    n = a_ref.shape[0]
    nb = n // NB
    s_ref[...] = a_ref[...]
    b_ref[...] = jnp.zeros_like(b_ref)
    x_ref[...] = jnp.zeros_like(x_ref)

    @pl.loop(0, nb)
    def _(k):
        rows = pl.ds(pl.multiple_of(k * NB, NB), NB)
        for g, v in enumerate(elim(lambda g: s_ref[pl.ds(pl.multiple_of(k * NB + 8 * g, 8), 8), rows])):
            w_ref[pl.ds(8 * g, 8), :] = v
        w = w_ref[...]
        u = exact_dot(w, s_ref[rows, :], ((1,), (0,)))
        x_ref[rows, :] = exact_dot(w, b_ref[rows, :], ((1,), (0,)))
        x_ref[rows, rows] = w

        @pl.loop(k + 1, nb)
        def _(i):
            below = pl.ds(pl.multiple_of(i * NB, NB), NB)
            ui = exact_dot(w, s_ref[rows, below], ((1,), (0,)))
            s_ref[below, :] -= exact_dot(ui, u, ((0,), (0,)))
            b_ref[below, :] -= exact_dot(ui, x_ref[rows, :], ((0,), (0,)))


def chol_kernel(a_ref, x_ref, w_ref, s_ref, b_ref, ah_ref, al_ref, yh_ref, yl_ref, e_ref, d_ref):
    n = a_ref.shape[0]
    nb = n // NB
    eye = (lax.broadcasted_iota(jnp.int32, (NB, NB), 0) == lax.broadcasted_iota(jnp.int32, (NB, NB), 1)).astype(F32)
    lower = (lax.broadcasted_iota(jnp.int32, (NB, NB), 0) > lax.broadcasted_iota(jnp.int32, (NB, NB), 1)).astype(F32) + 0.5 * eye

    for r in range(nb):
        at = pl.ds(r * NB, NB)
        d_ref[:, at] = lax.rsqrt(jnp.sum(a_ref[at, at] * eye, axis=0, keepdims=True))
    for r in range(nb):
        at = pl.ds(r * NB, NB)
        here = jnp.sum(eye * d_ref[:, at], axis=1, keepdims=True)
        hi, lo = halves(a_ref[at, :] * here * d_ref[...])
        ah_ref[at, :] = hi
        al_ref[at, :] = lo
    x_ref[...] = jnp.zeros_like(x_ref)
    yh_ref[...] = jnp.zeros_like(yh_ref)
    yl_ref[...] = jnp.zeros_like(yl_ref)
    for r in range(nb):
        at = pl.ds(r * NB, NB)
        end = (r + 1) * NB
        a = ah_ref[at, :end].astype(F32)
        if r:
            x_ref[at, : r * NB] = -a[:, : r * NB]
        x_ref[at, at] = eye - (a[:, r * NB :] - eye) * lower

    def step(fine):
        for r in range(nb):
            at, end = pl.ds(r * NB, NB), (r + 1) * NB
            hi, lo = halves(x_ref[at, :end])
            yh_ref[at, :end] = hi
            if fine:
                yl_ref[at, :end] = lo
        total = jnp.zeros((1, 1), F32)
        for r in range(nb):
            at, start, end = pl.ds(r * NB, NB), r * NB, (r + 1) * NB
            yh = yh_ref[at, :end]
            t = fast_dot(yh, ah_ref[:end, :end], ((1,), (0,)))
            if fine:
                t += fast_dot(yh, al_ref[:end, :end], ((1,), (0,))) + fast_dot(yl_ref[at, :end], ah_ref[:end, :end], ((1,), (0,)))
            hi, lo = halves(t)
            e = fast_dot(hi, yh_ref[:end, :end], ((1,), (1,)))
            if fine:
                e += fast_dot(lo, yh_ref[:end, :end], ((1,), (1,))) + fast_dot(hi, yl_ref[:end, :end], ((1,), (1,)))
            corner = (e[:, start:] - eye) * lower
            total += jnp.sum(corner * corner, keepdims=True)
            e_ref[at, start:end] = corner.astype(BF)
            if r:
                left = e[:, :start]
                total += jnp.sum(left * left, keepdims=True)
                e_ref[at, :start] = left.astype(BF)
        for r in reversed(range(nb)):
            at, end = pl.ds(r * NB, NB), (r + 1) * NB
            x_ref[at, :end] -= fast_dot(e_ref[at, :end], yh_ref[:end, :end], ((1,), (0,)))
        return total[0, 0]

    def more(tol, most):
        return lambda state: jnp.logical_and(state[0] < most, state[1] > tol)

    _, size = lax.while_loop(more(0.05, 10), lambda s: (s[0] + 1, step(False)), (0, jnp.float32(1e9)))
    _, size = lax.while_loop(more(1e-5, 6), lambda s: (s[0] + 1, step(True)), (0, jnp.float32(1e9)))
    good = size <= 1e-5

    @pl.when(good)
    def _():
        for r in range(nb):
            at, end = pl.ds(r * NB, NB), (r + 1) * NB
            x_ref[at, :end] *= d_ref[:, :end]

    @pl.when(jnp.logical_not(good))
    def _():
        eliminate(a_ref, x_ref, w_ref, s_ref, b_ref)


def chol_inv(a):
    n = a.shape[0]
    square = lambda kind: pltpu.VMEM((n, n), kind)
    return pl.pallas_call(
        chol_kernel,
        out_shape=jax.ShapeDtypeStruct((n, n), F32),
        in_specs=[pl.BlockSpec(memory_space=pltpu.VMEM)],
        out_specs=pl.BlockSpec(memory_space=pltpu.VMEM),
        scratch_shapes=[pltpu.VMEM((NB, NB), F32), square(F32), square(F32), square(BF), square(BF), square(BF), square(BF), square(BF), pltpu.VMEM((1, n), F32)],
        cost_estimate=pl.CostEstimate(flops=10**6, bytes_accessed=2**10, transcendentals=0),
        compiler_params=pltpu.CompilerParams(vmem_limit_bytes=32 * 2**20),
    )(a)


def mm(a, b, ca, cb):
    return lax.dot_general(a, b, (((ca,), (cb,)), ((), ())), preferred_element_type=F32)


def mm_split(a, b, ca, cb):
    hi = b.astype(BF)
    lo = (b - hi.astype(F32)).astype(BF)
    return mm(a, hi, ca, cb) + mm(a, lo, ca, cb)


def mm_high(a, b, ca, cb):
    return lax.dot_general(a, b, (((ca,), (cb,)), ((), ())), precision=lax.Precision.HIGH, preferred_element_type=F32)


def scatter_sum(x, axis, n):
    parts = lax.all_to_all(x.astype(BF).reshape(n, x.shape[0] // n, x.shape[1]), axis, 0, 0, tiled=True)
    return jnp.sum(parts.astype(F32), axis=0)


def gather(x, axis, n):
    parts = lax.all_to_all(jnp.broadcast_to(x[None], (n,) + x.shape), axis, 0, 0, tiled=True)
    return parts.reshape(n * x.shape[0], x.shape[1])


def row_major(x):
    return with_layout_constraint(x, Layout(tuple(range(x.ndim))))


def tiles(x):
    n, rows, cols = x.shape
    return x.reshape(n, rows // 8, 8, cols // 128, 128).transpose(0, 1, 3, 2, 4).reshape(n, -1, 128)


def finish_kernel(scale, parts_ref, high_ref, low_ref, one_ref, two_ref, out_ref):
    nf, rows, rank = parts_ref.shape
    share = rank // nf
    raw = parts_ref[0].astype(F32)
    for g in range(1, nf):
        raw += parts_ref[g].astype(F32)
    hi, lo = halves(raw)
    dims = ((1,), (1,))
    reduced = (fast_dot(hi, high_ref[...], dims) + fast_dot(lo, high_ref[...], dims) + fast_dot(hi, low_ref[...], dims)) * scale
    one = BETA_ONE * one_ref[...] + (1.0 - BETA_ONE) * reduced
    two = BETA_TWO * two_ref[...] + (1.0 - BETA_TWO) * reduced * reduced
    direction = (one / (jnp.sqrt(two) + ADAM_EPS)).astype(BF)
    pad = jnp.zeros((-rows % 128, rank), F32)
    one = jnp.concatenate([one, pad], axis=0).T
    two = jnp.concatenate([two, pad], axis=0).T
    both = [one.astype(BF), two.astype(BF)]
    for g in range(nf):
        out_ref[g, 16:, :] = direction
        for i in range(2 * share // 16):
            first = g * share + i * 16 % share
            out_ref[g, :16, i * 128 : (i + 1) * 128] = both[i * 16 // share][first : first + 16]


def finish(scale, parts, high, low, one, two):
    nf, rows, rank = parts.shape
    return pl.pallas_call(
        functools.partial(finish_kernel, scale),
        out_shape=jax.ShapeDtypeStruct((nf, 16 + rows, rank), BF),
        in_specs=[pl.BlockSpec(memory_space=pltpu.VMEM)] * 5,
        out_specs=pl.BlockSpec(memory_space=pltpu.VMEM),
        cost_estimate=pl.CostEstimate(flops=10**9, bytes_accessed=6 * 2**20, transcendentals=0),
        compiler_params=pltpu.CompilerParams(vmem_limit_bytes=32 * 2**20),
    )(parts, high, low, one, two)


def unpack_kernel(width, got_ref, one_ref, two_ref):
    share = one_ref.shape[0]
    for ref, first in ((one_ref, 0), (two_ref, share)):
        for i in range(share // 16):
            lanes = slice((first // 16 + i) * 128, (first // 16 + i) * 128 + width)
            rows = [got_ref[g].astype(F32)[:, lanes] for g in range(got_ref.shape[0])]
            ref[i * 16 : (i + 1) * 16, :] = jnp.concatenate(rows, axis=1)


def unpack(got, width, share):
    shape = jax.ShapeDtypeStruct((share, got.shape[0] * width), F32)
    return pl.pallas_call(
        functools.partial(unpack_kernel, width),
        out_shape=[shape, shape],
        in_specs=[pl.BlockSpec(memory_space=pltpu.VMEM)],
        out_specs=[pl.BlockSpec(memory_space=pltpu.VMEM)] * 2,
        cost_estimate=pl.CostEstimate(flops=10**6, bytes_accessed=2**20, transcendentals=0),
    )(got)


def per_device(nf, nt, grad, start_basis, weight, first_moment, second_moment):
    inv_sqrt = 1.0 / math.sqrt(M)
    share_rows, cols = first_moment.shape
    share_cols = cols // nf
    rank = start_basis.shape[1]

    sent = jnp.concatenate([first_moment.astype(BF), second_moment.astype(BF)], axis=0)
    sent = sent.reshape(2 * share_rows, nf, share_cols).transpose(1, 0, 2)
    sent = row_major(jnp.pad(sent, ((0, 0), (0, 0), (0, -share_cols % 128))))

    first_row = (lax.axis_index("fsdp") * (rank // nf)).astype(jnp.uint32)
    panel, first_row = lax.optimization_barrier((mm(grad, start_basis, 0, 0).astype(BF), first_row))
    panel = (scatter_sum(panel, "fsdp", nf) * inv_sqrt).astype(BF)
    panel = gather(panel, "fsdp", nf)
    image = scatter_sum(mm(grad, panel, 1, 0), "tp", nt).astype(BF)
    image = lax.all_gather(image, "tp", axis=0, tiled=True)
    raw = scatter_sum(row_major(mm(grad, image, 0, 0).astype(BF)), "fsdp", nf).astype(BF)

    raw = gather(raw, "fsdp", nf)
    rows = rank // nt
    few = rank // nf // nt
    mine = lax.dynamic_slice(mm(panel, raw, 0, 0), (first_row, jnp.uint32(0)), (rank // nf, rank))
    mine = jnp.pad(mine.astype(BF).reshape(nt, few, rank), ((0, 0), (0, -few % 8), (0, 0)))
    both = jnp.concatenate([mm(grad, raw, 1, 0).astype(BF).reshape(nt, rows, rank), mine], axis=1)
    both = jnp.sum(lax.all_to_all(both, "tp", 0, 0, tiled=True).astype(F32), axis=0).astype(BF)
    both = lax.all_gather(both, "tp", axis=0, tiled=False)
    wide = both[:, :rows].reshape(-1, rank)
    gram = both[:, rows : rows + few].reshape(1, rank // nf, rank)
    outer = (mm(wide, wide, 0, 0) / M).astype(BF).reshape(nf, -1, rank)
    raw = row_major(mm(grad, wide, 0, 0).astype(BF))
    got = jnp.concatenate([sent, tiles(outer)], axis=1)
    got = lax.all_to_all(got, "fsdp", 0, 0, tiled=True)
    first_old = got[:, :share_rows].reshape(rank, -1)
    second_old = got[:, share_rows : 2 * share_rows].reshape(rank, -1)
    sums = jnp.sum(got[:, 2 * share_rows :].astype(F32), axis=0).astype(BF)
    grams = gather(jnp.concatenate([sums, tiles(gram)[0]], axis=0), "fsdp", nf)
    grams, raw = lax.optimization_barrier((grams, raw))
    grams = grams.reshape(nf, 2, -1, rank // 128, 8, 128).transpose(1, 0, 2, 4, 3, 5).reshape(2, rank, rank)
    outer, gram = grams[0].astype(F32), grams[1].astype(F32) / M
    inverse = chol_inv(gram)
    second = chol_inv(mm_high(mm_high(inverse, outer, 1, 0), inverse, 1, 1) / M)
    both = mm_high(second, inverse, 1, 0)
    margin = mm_high(gram, both, 0, 1)
    first_basis = mm_split(image, inverse, 1, 1).astype(BF)
    new_basis = (mm_split(wide, both, 1, 1) * inv_sqrt).astype(BF)
    rotated_one = mm(first_old, margin.astype(BF), 0, 0)[:share_cols]
    rotated_two = mm(second_old, (margin * margin).astype(BF), 0, 0)[:share_cols]
    parts = lax.all_to_all(raw.reshape(nf, share_cols, rank), "fsdp", 0, 0, tiled=True)
    rotated_one, rotated_two, first_basis, new_basis = lax.optimization_barrier(
        (rotated_one, rotated_two, first_basis, new_basis)
    )
    got = finish(1.0 / M, parts, *halves(both), rotated_one, rotated_two)
    got = lax.all_to_all(got, "fsdp", 0, 0, tiled=True)
    direction = got[:, 16:].reshape(cols, rank)
    moment_one, moment_two = unpack(got[:, :16], share_cols, share_rows)
    expanded = mm(new_basis, direction, 1, 1)
    new_weight = (weight.astype(F32) - STEP_SIZE * inv_sqrt * expanded).astype(BF)
    return (first_basis, new_basis, moment_one, moment_two, new_weight)


def solution(mesh):
    specs = (P("fsdp", "tp"), P("fsdp", None), P("fsdp", "tp"), P("fsdp", "tp"), P("fsdp", "tp"))
    out_specs = (P("fsdp", None), P("fsdp", None), P("fsdp", "tp"), P("fsdp", "tp"), P("fsdp", "tp"))
    nf, nt = mesh.shape["fsdp"], mesh.shape["tp"]

    def body(*args):
        return per_device(nf, nt, *args)

    return jax.shard_map(body, mesh=mesh, in_specs=specs, out_specs=out_specs, check_vma=False)
```

```python
import functools
import math

import jax
import jax.numpy as jnp
from jax import lax
from jax.experimental import pallas as pl
from jax.experimental.pallas import tpu as pltpu
from jax.experimental.layout import Layout, with_layout_constraint
from jax.sharding import PartitionSpec as P

M = 8192

BETA_ONE = 0.9
BETA_TWO = 0.95
ADAM_EPS = 1e-06
STEP_SIZE = 2.0

BF = jnp.bfloat16
F32 = jnp.float32

def elim(read, n=128):
    lane = lax.broadcasted_iota(jnp.int32, (8, n), 1)
    sub = lax.broadcasted_iota(jnp.int32, (8, n), 0)
    G = [read(g) for g in range(n // 8)]
    out = []
    for g0 in range(n // 8):
        acc = jnp.zeros((8, n), jnp.float32)
        for s0 in range(8):
            j = g0 * 8 + s0
            hit = lane == j
            r = jnp.broadcast_to(G[g0][s0:s0 + 1, :], (8, n))
            p = jnp.broadcast_to(r[:, j:j + 1], (8, n))
            row = jnp.where(lane < j, r, jnp.where(hit, 1.0, 0.0)) * lax.rsqrt(p)
            acc = jnp.where(sub == s0, row, acc)
            rr = jnp.where(hit, 1.0, r) * (1.0 / p)
            for g in range(g0, n // 8):
                c = jnp.broadcast_to(G[g][:, j:j + 1], (8, n))
                new = jnp.where(hit, 0.0, G[g]) - c * rr
                G[g] = jnp.where(sub > s0, new, G[g]) if g == g0 else new
        out.append(acc)
    return out


NB = 128


def exact_dot(a, b, dims):
    return lax.dot_general(a, b, (dims, ((), ())), precision=lax.Precision.HIGHEST, preferred_element_type=F32)


def fast_dot(a, b, dims):
    return lax.dot_general(a, b, (dims, ((), ())), preferred_element_type=F32)


def halves(x):
    hi = x.astype(BF)
    return hi, (x - hi.astype(F32)).astype(BF)


def eliminate(a_ref, x_ref, w_ref, s_ref, b_ref):
    n = a_ref.shape[0]
    nb = n // NB
    s_ref[...] = a_ref[...]
    b_ref[...] = jnp.zeros_like(b_ref)
    x_ref[...] = jnp.zeros_like(x_ref)

    @pl.loop(0, nb)
    def _(k):
        rows = pl.ds(pl.multiple_of(k * NB, NB), NB)
        for g, v in enumerate(elim(lambda g: s_ref[pl.ds(pl.multiple_of(k * NB + 8 * g, 8), 8), rows])):
            w_ref[pl.ds(8 * g, 8), :] = v
        w = w_ref[...]
        u = exact_dot(w, s_ref[rows, :], ((1,), (0,)))
        x_ref[rows, :] = exact_dot(w, b_ref[rows, :], ((1,), (0,)))
        x_ref[rows, rows] = w

        @pl.loop(k + 1, nb)
        def _(i):
            below = pl.ds(pl.multiple_of(i * NB, NB), NB)
            ui = exact_dot(w, s_ref[rows, below], ((1,), (0,)))
            s_ref[below, :] -= exact_dot(ui, u, ((0,), (0,)))
            b_ref[below, :] -= exact_dot(ui, x_ref[rows, :], ((0,), (0,)))


def chol_kernel(a_ref, x_ref, w_ref, s_ref, b_ref, ah_ref, al_ref, yh_ref, yl_ref, e_ref, d_ref):
    n = a_ref.shape[0]
    nb = n // NB
    eye = (lax.broadcasted_iota(jnp.int32, (NB, NB), 0) == lax.broadcasted_iota(jnp.int32, (NB, NB), 1)).astype(F32)
    lower = (lax.broadcasted_iota(jnp.int32, (NB, NB), 0) > lax.broadcasted_iota(jnp.int32, (NB, NB), 1)).astype(F32) + 0.5 * eye

    for r in range(nb):
        at = pl.ds(r * NB, NB)
        d_ref[:, at] = lax.rsqrt(jnp.sum(a_ref[at, at] * eye, axis=0, keepdims=True))
    for r in range(nb):
        at = pl.ds(r * NB, NB)
        here = jnp.sum(eye * d_ref[:, at], axis=1, keepdims=True)
        hi, lo = halves(a_ref[at, :] * here * d_ref[...])
        ah_ref[at, :] = hi
        al_ref[at, :] = lo
    x_ref[...] = jnp.zeros_like(x_ref)
    yh_ref[...] = jnp.zeros_like(yh_ref)
    yl_ref[...] = jnp.zeros_like(yl_ref)
    for r in range(nb):
        at = pl.ds(r * NB, NB)
        end = (r + 1) * NB
        a = ah_ref[at, :end].astype(F32)
        if r:
            x_ref[at, : r * NB] = -a[:, : r * NB]
        x_ref[at, at] = eye - (a[:, r * NB :] - eye) * lower

    def step(fine):
        for r in range(nb):
            at, end = pl.ds(r * NB, NB), (r + 1) * NB
            hi, lo = halves(x_ref[at, :end])
            yh_ref[at, :end] = hi
            if fine:
                yl_ref[at, :end] = lo
        total = jnp.zeros((1, 1), F32)
        for r in range(nb):
            at, start, end = pl.ds(r * NB, NB), r * NB, (r + 1) * NB
            yh = yh_ref[at, :end]
            t = fast_dot(yh, ah_ref[:end, :end], ((1,), (0,)))
            if fine:
                t += fast_dot(yh, al_ref[:end, :end], ((1,), (0,))) + fast_dot(yl_ref[at, :end], ah_ref[:end, :end], ((1,), (0,)))
            hi, lo = halves(t)
            e = fast_dot(hi, yh_ref[:end, :end], ((1,), (1,)))
            if fine:
                e += fast_dot(lo, yh_ref[:end, :end], ((1,), (1,))) + fast_dot(hi, yl_ref[:end, :end], ((1,), (1,)))
            corner = (e[:, start:] - eye) * lower
            total += jnp.sum(corner * corner, keepdims=True)
            e_ref[at, start:end] = corner.astype(BF)
            if r:
                left = e[:, :start]
                total += jnp.sum(left * left, keepdims=True)
                e_ref[at, :start] = left.astype(BF)
        for r in reversed(range(nb)):
            at, end = pl.ds(r * NB, NB), (r + 1) * NB
            x_ref[at, :end] -= fast_dot(e_ref[at, :end], yh_ref[:end, :end], ((1,), (0,)))
        return total[0, 0]

    def more(tol, most):
        return lambda state: jnp.logical_and(state[0] < most, state[1] > tol)

    _, size = lax.while_loop(more(0.05, 10), lambda s: (s[0] + 1, step(False)), (0, jnp.float32(1e9)))
    _, size = lax.while_loop(more(1e-5, 6), lambda s: (s[0] + 1, step(True)), (0, jnp.float32(1e9)))
    good = size <= 1e-5

    @pl.when(good)
    def _():
        for r in range(nb):
            at, end = pl.ds(r * NB, NB), (r + 1) * NB
            x_ref[at, :end] *= d_ref[:, :end]

    @pl.when(jnp.logical_not(good))
    def _():
        eliminate(a_ref, x_ref, w_ref, s_ref, b_ref)


def chol_inv(a):
    n = a.shape[0]
    square = lambda kind: pltpu.VMEM((n, n), kind)
    return pl.pallas_call(
        chol_kernel,
        out_shape=jax.ShapeDtypeStruct((n, n), F32),
        in_specs=[pl.BlockSpec(memory_space=pltpu.VMEM)],
        out_specs=pl.BlockSpec(memory_space=pltpu.VMEM),
        scratch_shapes=[pltpu.VMEM((NB, NB), F32), square(F32), square(F32), square(BF), square(BF), square(BF), square(BF), square(BF), pltpu.VMEM((1, n), F32)],
        cost_estimate=pl.CostEstimate(flops=10**6, bytes_accessed=2**10, transcendentals=0),
        compiler_params=pltpu.CompilerParams(vmem_limit_bytes=32 * 2**20),
    )(a)


def mm(a, b, ca, cb):
    return lax.dot_general(a, b, (((ca,), (cb,)), ((), ())), preferred_element_type=F32)


def mm_split(a, b, ca, cb):
    hi = b.astype(BF)
    lo = (b - hi.astype(F32)).astype(BF)
    return mm(a, hi, ca, cb) + mm(a, lo, ca, cb)


def mm_high(a, b, ca, cb):
    return lax.dot_general(a, b, (((ca,), (cb,)), ((), ())), precision=lax.Precision.HIGH, preferred_element_type=F32)


def scatter_sum(x, axis, n):
    parts = lax.all_to_all(x.astype(BF).reshape(n, x.shape[0] // n, x.shape[1]), axis, 0, 0, tiled=True)
    return jnp.sum(parts.astype(F32), axis=0)


def gather(x, axis, n):
    parts = lax.all_to_all(jnp.broadcast_to(x[None], (n,) + x.shape), axis, 0, 0, tiled=True)
    return parts.reshape(n * x.shape[0], x.shape[1])


def row_major(x):
    return with_layout_constraint(x, Layout(tuple(range(x.ndim))))


def tiles(x):
    n, rows, cols = x.shape
    return x.reshape(n, rows // 8, 8, cols // 128, 128).transpose(0, 1, 3, 2, 4).reshape(n, -1, 128)


def finish_kernel(scale, parts_ref, high_ref, low_ref, one_ref, two_ref, out_ref):
    nf, rows, rank = parts_ref.shape
    share = rank // nf
    raw = parts_ref[0].astype(F32)
    for g in range(1, nf):
        raw += parts_ref[g].astype(F32)
    hi, lo = halves(raw)
    dims = ((1,), (1,))
    reduced = (fast_dot(hi, high_ref[...], dims) + fast_dot(lo, high_ref[...], dims) + fast_dot(hi, low_ref[...], dims)) * scale
    one = BETA_ONE * one_ref[...] + (1.0 - BETA_ONE) * reduced
    two = BETA_TWO * two_ref[...] + (1.0 - BETA_TWO) * reduced * reduced
    direction = (one / (jnp.sqrt(two) + ADAM_EPS)).astype(BF)
    pad = jnp.zeros((-rows % 128, rank), F32)
    one = jnp.concatenate([one, pad], axis=0).T
    two = jnp.concatenate([two, pad], axis=0).T
    both = [one.astype(BF), two.astype(BF)]
    for g in range(nf):
        out_ref[g, 16:, :] = direction
        for i in range(2 * share // 16):
            first = g * share + i * 16 % share
            out_ref[g, :16, i * 128 : (i + 1) * 128] = both[i * 16 // share][first : first + 16]


def finish(scale, parts, high, low, one, two):
    nf, rows, rank = parts.shape
    return pl.pallas_call(
        functools.partial(finish_kernel, scale),
        out_shape=jax.ShapeDtypeStruct((nf, 16 + rows, rank), BF),
        in_specs=[pl.BlockSpec(memory_space=pltpu.VMEM)] * 5,
        out_specs=pl.BlockSpec(memory_space=pltpu.VMEM),
        cost_estimate=pl.CostEstimate(flops=10**9, bytes_accessed=6 * 2**20, transcendentals=0),
        compiler_params=pltpu.CompilerParams(vmem_limit_bytes=32 * 2**20),
    )(parts, high, low, one, two)


def unpack_kernel(width, got_ref, one_ref, two_ref):
    share = one_ref.shape[0]
    for ref, first in ((one_ref, 0), (two_ref, share)):
        for i in range(share // 16):
            lanes = slice((first // 16 + i) * 128, (first // 16 + i) * 128 + width)
            rows = [got_ref[g].astype(F32)[:, lanes] for g in range(got_ref.shape[0])]
            ref[i * 16 : (i + 1) * 16, :] = jnp.concatenate(rows, axis=1)


def unpack(got, width, share):
    shape = jax.ShapeDtypeStruct((share, got.shape[0] * width), F32)
    return pl.pallas_call(
        functools.partial(unpack_kernel, width),
        out_shape=[shape, shape],
        in_specs=[pl.BlockSpec(memory_space=pltpu.VMEM)],
        out_specs=[pl.BlockSpec(memory_space=pltpu.VMEM)] * 2,
        cost_estimate=pl.CostEstimate(flops=10**6, bytes_accessed=2**20, transcendentals=0),
    )(got)


def per_device(nf, nt, grad, start_basis, weight, first_moment, second_moment):
    inv_sqrt = 1.0 / math.sqrt(M)
    share_rows, cols = first_moment.shape
    share_cols = cols // nf
    rank = start_basis.shape[1]

    sent = jnp.concatenate([first_moment.astype(BF), second_moment.astype(BF)], axis=0)
    sent = sent.reshape(2 * share_rows, nf, share_cols).transpose(1, 0, 2)
    sent = row_major(jnp.pad(sent, ((0, 0), (0, 0), (0, -share_cols % 128))))

    first_row = (lax.axis_index("fsdp") * (rank // nf)).astype(jnp.uint32)
    panel, first_row = lax.optimization_barrier((mm(grad, start_basis, 0, 0).astype(BF), first_row))
    panel = (scatter_sum(panel, "fsdp", nf) * inv_sqrt).astype(BF)
    panel = gather(panel, "fsdp", nf)
    image = scatter_sum(mm(grad, panel, 1, 0), "tp", nt).astype(BF)
    image = lax.all_gather(image, "tp", axis=0, tiled=True)
    raw = scatter_sum(row_major(mm(grad, image, 0, 0).astype(BF)), "fsdp", nf).astype(BF)

    raw = gather(raw, "fsdp", nf)
    rows = rank // nt
    few = rank // nf // nt
    mine = lax.dynamic_slice(mm(panel, raw, 0, 0), (first_row, jnp.uint32(0)), (rank // nf, rank))
    mine = jnp.pad(mine.astype(BF).reshape(nt, few, rank), ((0, 0), (0, -few % 8), (0, 0)))
    both = jnp.concatenate([mm(grad, raw, 1, 0).astype(BF).reshape(nt, rows, rank), mine], axis=1)
    both = jnp.sum(lax.all_to_all(both, "tp", 0, 0, tiled=True).astype(F32), axis=0).astype(BF)
    both = lax.all_gather(both, "tp", axis=0, tiled=False)
    wide = both[:, :rows].reshape(-1, rank)
    gram = both[:, rows : rows + few].reshape(1, rank // nf, rank)
    outer = (mm(wide, wide, 0, 0) / M).astype(BF).reshape(nf, -1, rank)
    raw = row_major(mm(grad, wide, 0, 0).astype(BF))
    gram = jnp.broadcast_to(tiles(gram), (nf, rank * rank // nf // 128, 128))
    got = jnp.concatenate([sent, tiles(outer), gram], axis=1)
    got = lax.all_to_all(got, "fsdp", 0, 0, tiled=True)
    first_old = got[:, :share_rows].reshape(rank, -1)
    second_old = got[:, share_rows : 2 * share_rows].reshape(rank, -1)
    gram = got[:, 2 * share_rows + gram.shape[1] :]
    sums = jnp.sum(got[:, 2 * share_rows : -gram.shape[1]].astype(F32), axis=0).astype(BF)
    outer, raw = lax.optimization_barrier((gather(sums, "fsdp", nf), raw))
    outer, gram = [x.reshape(-1, rank // 128, 8, 128).transpose(0, 2, 1, 3).reshape(rank, rank).astype(F32) for x in (outer, gram)]
    gram = gram / M
    inverse = chol_inv(gram)
    second = chol_inv(mm_high(mm_high(inverse, outer, 1, 0), inverse, 1, 1) / M)
    both = mm_high(second, inverse, 1, 0)
    margin = mm_high(gram, both, 0, 1)
    first_basis = mm_split(image, inverse, 1, 1).astype(BF)
    new_basis = (mm_split(wide, both, 1, 1) * inv_sqrt).astype(BF)
    rotated_one = mm(first_old, margin.astype(BF), 0, 0)[:share_cols]
    rotated_two = mm(second_old, (margin * margin).astype(BF), 0, 0)[:share_cols]
    parts = lax.all_to_all(raw.reshape(nf, share_cols, rank), "fsdp", 0, 0, tiled=True)
    rotated_one, rotated_two, first_basis, new_basis = lax.optimization_barrier(
        (rotated_one, rotated_two, first_basis, new_basis)
    )
    got = finish(1.0 / M, parts, *halves(both), rotated_one, rotated_two)
    got = lax.all_to_all(got, "fsdp", 0, 0, tiled=True)
    direction = got[:, 16:].reshape(cols, rank)
    moment_one, moment_two = unpack(got[:, :16], share_cols, share_rows)
    expanded = mm(new_basis, direction, 1, 1)
    new_weight = (weight.astype(F32) - STEP_SIZE * inv_sqrt * expanded).astype(BF)
    return (first_basis, new_basis, moment_one, moment_two, new_weight)


def solution(mesh):
    specs = (P("fsdp", "tp"), P("fsdp", None), P("fsdp", "tp"), P("fsdp", "tp"), P("fsdp", "tp"))
    out_specs = (P("fsdp", None), P("fsdp", None), P("fsdp", "tp"), P("fsdp", "tp"), P("fsdp", "tp"))
    nf, nt = mesh.shape["fsdp"], mesh.shape["tp"]

    def body(*args):
        return per_device(nf, nt, *args)

    return jax.shard_map(body, mesh=mesh, in_specs=specs, out_specs=out_specs, check_vma=False)
```

```python
import functools
import math

import jax
import jax.numpy as jnp
from jax import lax
from jax.experimental import pallas as pl
from jax.experimental.pallas import tpu as pltpu
from jax.experimental.layout import Layout, with_layout_constraint
from jax.sharding import PartitionSpec as P

M = 8192

BETA_ONE = 0.9
BETA_TWO = 0.95
ADAM_EPS = 1e-06
STEP_SIZE = 2.0

BF = jnp.bfloat16
F32 = jnp.float32

def elim(read, n=128):
    lane = lax.broadcasted_iota(jnp.int32, (8, n), 1)
    sub = lax.broadcasted_iota(jnp.int32, (8, n), 0)
    G = [read(g) for g in range(n // 8)]
    out = []
    for g0 in range(n // 8):
        acc = jnp.zeros((8, n), jnp.float32)
        for s0 in range(8):
            j = g0 * 8 + s0
            hit = lane == j
            r = jnp.broadcast_to(G[g0][s0:s0 + 1, :], (8, n))
            p = jnp.broadcast_to(r[:, j:j + 1], (8, n))
            row = jnp.where(lane < j, r, jnp.where(hit, 1.0, 0.0)) * lax.rsqrt(p)
            acc = jnp.where(sub == s0, row, acc)
            rr = jnp.where(hit, 1.0, r) * (1.0 / p)
            for g in range(g0, n // 8):
                c = jnp.broadcast_to(G[g][:, j:j + 1], (8, n))
                new = jnp.where(hit, 0.0, G[g]) - c * rr
                G[g] = jnp.where(sub > s0, new, G[g]) if g == g0 else new
        out.append(acc)
    return out


NB = 128


def exact_dot(a, b, dims):
    return lax.dot_general(a, b, (dims, ((), ())), precision=lax.Precision.HIGHEST, preferred_element_type=F32)


def fast_dot(a, b, dims):
    return lax.dot_general(a, b, (dims, ((), ())), preferred_element_type=F32)


def halves(x):
    hi = x.astype(BF)
    return hi, (x - hi.astype(F32)).astype(BF)


def eliminate(a_ref, x_ref, w_ref, s_ref, b_ref):
    n = a_ref.shape[0]
    nb = n // NB
    s_ref[...] = a_ref[...]
    b_ref[...] = jnp.zeros_like(b_ref)
    x_ref[...] = jnp.zeros_like(x_ref)

    @pl.loop(0, nb)
    def _(k):
        rows = pl.ds(pl.multiple_of(k * NB, NB), NB)
        for g, v in enumerate(elim(lambda g: s_ref[pl.ds(pl.multiple_of(k * NB + 8 * g, 8), 8), rows])):
            w_ref[pl.ds(8 * g, 8), :] = v
        w = w_ref[...]
        u = exact_dot(w, s_ref[rows, :], ((1,), (0,)))
        x_ref[rows, :] = exact_dot(w, b_ref[rows, :], ((1,), (0,)))
        x_ref[rows, rows] = w

        @pl.loop(k + 1, nb)
        def _(i):
            below = pl.ds(pl.multiple_of(i * NB, NB), NB)
            ui = exact_dot(w, s_ref[rows, below], ((1,), (0,)))
            s_ref[below, :] -= exact_dot(ui, u, ((0,), (0,)))
            b_ref[below, :] -= exact_dot(ui, x_ref[rows, :], ((0,), (0,)))


def chol_kernel(a_ref, x_ref, w_ref, s_ref, b_ref, ah_ref, al_ref, yh_ref, yl_ref, e_ref, d_ref):
    n = a_ref.shape[0]
    nb = n // NB
    eye = (lax.broadcasted_iota(jnp.int32, (NB, NB), 0) == lax.broadcasted_iota(jnp.int32, (NB, NB), 1)).astype(F32)
    lower = (lax.broadcasted_iota(jnp.int32, (NB, NB), 0) > lax.broadcasted_iota(jnp.int32, (NB, NB), 1)).astype(F32) + 0.5 * eye

    for r in range(nb):
        at = pl.ds(r * NB, NB)
        d_ref[:, at] = lax.rsqrt(jnp.sum(a_ref[at, at] * eye, axis=0, keepdims=True))
    for r in range(nb):
        at = pl.ds(r * NB, NB)
        here = jnp.sum(eye * d_ref[:, at], axis=1, keepdims=True)
        hi, lo = halves(a_ref[at, :] * here * d_ref[...])
        ah_ref[at, :] = hi
        al_ref[at, :] = lo
    x_ref[...] = jnp.zeros_like(x_ref)
    yh_ref[...] = jnp.zeros_like(yh_ref)
    yl_ref[...] = jnp.zeros_like(yl_ref)
    for r in range(nb):
        at = pl.ds(r * NB, NB)
        end = (r + 1) * NB
        a = ah_ref[at, :end].astype(F32)
        if r:
            x_ref[at, : r * NB] = -a[:, : r * NB]
        x_ref[at, at] = eye - (a[:, r * NB :] - eye) * lower

    def step(fine):
        for r in range(nb):
            at, end = pl.ds(r * NB, NB), (r + 1) * NB
            hi, lo = halves(x_ref[at, :end])
            yh_ref[at, :end] = hi
            if fine:
                yl_ref[at, :end] = lo
        total = jnp.zeros((1, 1), F32)
        for r in range(nb):
            at, start, end = pl.ds(r * NB, NB), r * NB, (r + 1) * NB
            yh = yh_ref[at, :end]
            t = fast_dot(yh, ah_ref[:end, :end], ((1,), (0,)))
            if fine:
                t += fast_dot(yh, al_ref[:end, :end], ((1,), (0,))) + fast_dot(yl_ref[at, :end], ah_ref[:end, :end], ((1,), (0,)))
            hi, lo = halves(t)
            e = fast_dot(hi, yh_ref[:end, :end], ((1,), (1,)))
            if fine:
                e += fast_dot(lo, yh_ref[:end, :end], ((1,), (1,))) + fast_dot(hi, yl_ref[:end, :end], ((1,), (1,)))
            corner = (e[:, start:] - eye) * lower
            total += jnp.sum(corner * corner, keepdims=True)
            e_ref[at, start:end] = corner.astype(BF)
            if r:
                left = e[:, :start]
                total += jnp.sum(left * left, keepdims=True)
                e_ref[at, :start] = left.astype(BF)
        for r in reversed(range(nb)):
            at, end = pl.ds(r * NB, NB), (r + 1) * NB
            x_ref[at, :end] -= fast_dot(e_ref[at, :end], yh_ref[:end, :end], ((1,), (0,)))
        return total[0, 0]

    def more(tol, most):
        return lambda state: jnp.logical_and(state[0] < most, state[1] > tol)

    _, size = lax.while_loop(more(0.05, 10), lambda s: (s[0] + 1, step(False)), (0, jnp.float32(1e9)))
    _, size = lax.while_loop(more(1e-5, 6), lambda s: (s[0] + 1, step(True)), (0, jnp.float32(1e9)))
    good = size <= 1e-5

    @pl.when(good)
    def _():
        for r in range(nb):
            at, end = pl.ds(r * NB, NB), (r + 1) * NB
            x_ref[at, :end] *= d_ref[:, :end]

    @pl.when(jnp.logical_not(good))
    def _():
        eliminate(a_ref, x_ref, w_ref, s_ref, b_ref)


def chol_inv(a):
    n = a.shape[0]
    square = lambda kind: pltpu.VMEM((n, n), kind)
    return pl.pallas_call(
        chol_kernel,
        out_shape=jax.ShapeDtypeStruct((n, n), F32),
        in_specs=[pl.BlockSpec(memory_space=pltpu.VMEM)],
        out_specs=pl.BlockSpec(memory_space=pltpu.VMEM),
        scratch_shapes=[pltpu.VMEM((NB, NB), F32), square(F32), square(F32), square(BF), square(BF), square(BF), square(BF), square(BF), pltpu.VMEM((1, n), F32)],
        cost_estimate=pl.CostEstimate(flops=10**6, bytes_accessed=2**10, transcendentals=0),
        compiler_params=pltpu.CompilerParams(vmem_limit_bytes=32 * 2**20),
    )(a)


def mm(a, b, ca, cb):
    return lax.dot_general(a, b, (((ca,), (cb,)), ((), ())), preferred_element_type=F32)


def mm_split(a, b, ca, cb):
    hi = b.astype(BF)
    lo = (b - hi.astype(F32)).astype(BF)
    return mm(a, hi, ca, cb) + mm(a, lo, ca, cb)


def mm_high(a, b, ca, cb):
    return lax.dot_general(a, b, (((ca,), (cb,)), ((), ())), precision=lax.Precision.HIGH, preferred_element_type=F32)


def scatter_sum(x, axis, n):
    parts = lax.all_to_all(x.astype(BF).reshape(n, x.shape[0] // n, x.shape[1]), axis, 0, 0, tiled=True)
    return jnp.sum(parts.astype(F32), axis=0)


def gather(x, axis, n):
    parts = lax.all_to_all(jnp.broadcast_to(x[None], (n,) + x.shape), axis, 0, 0, tiled=True)
    return parts.reshape(n * x.shape[0], x.shape[1])


def row_major(x):
    return with_layout_constraint(x, Layout(tuple(range(x.ndim))))


def tiles(x):
    n, rows, cols = x.shape
    return x.reshape(n, rows // 8, 8, cols // 128, 128).transpose(0, 1, 3, 2, 4).reshape(n, -1, 128)


def finish_kernel(scale, parts_ref, high_ref, low_ref, one_ref, two_ref, out_ref):
    nf, rows, rank = parts_ref.shape
    share = rank // nf
    raw = parts_ref[0].astype(F32)
    for g in range(1, nf):
        raw += parts_ref[g].astype(F32)
    hi, lo = halves(raw)
    dims = ((1,), (1,))
    reduced = (fast_dot(hi, high_ref[...], dims) + fast_dot(lo, high_ref[...], dims) + fast_dot(hi, low_ref[...], dims)) * scale
    one = BETA_ONE * one_ref[...] + (1.0 - BETA_ONE) * reduced
    two = BETA_TWO * two_ref[...] + (1.0 - BETA_TWO) * reduced * reduced
    direction = (one / (jnp.sqrt(two) + ADAM_EPS)).astype(BF)
    pad = jnp.zeros((-rows % 128, rank), F32)
    one = jnp.concatenate([one, pad], axis=0).T
    two = jnp.concatenate([two, pad], axis=0).T
    both = [one.astype(BF), two.astype(BF)]
    for g in range(nf):
        out_ref[g, 16:, :] = direction
        for i in range(2 * share // 16):
            first = g * share + i * 16 % share
            out_ref[g, :16, i * 128 : (i + 1) * 128] = both[i * 16 // share][first : first + 16]


def finish(scale, parts, high, low, one, two):
    nf, rows, rank = parts.shape
    return pl.pallas_call(
        functools.partial(finish_kernel, scale),
        out_shape=jax.ShapeDtypeStruct((nf, 16 + rows, rank), BF),
        in_specs=[pl.BlockSpec(memory_space=pltpu.VMEM)] * 5,
        out_specs=pl.BlockSpec(memory_space=pltpu.VMEM),
        cost_estimate=pl.CostEstimate(flops=10**9, bytes_accessed=6 * 2**20, transcendentals=0),
        compiler_params=pltpu.CompilerParams(vmem_limit_bytes=32 * 2**20),
    )(parts, high, low, one, two)


def unpack_kernel(width, got_ref, one_ref, two_ref):
    share = one_ref.shape[0]
    for ref, first in ((one_ref, 0), (two_ref, share)):
        for i in range(share // 16):
            lanes = slice((first // 16 + i) * 128, (first // 16 + i) * 128 + width)
            rows = [got_ref[g, :16, :].astype(F32)[:, lanes] for g in range(got_ref.shape[0])]
            ref[i * 16 : (i + 1) * 16, :] = jnp.concatenate(rows, axis=1)


def unpack(got, width, share):
    shape = jax.ShapeDtypeStruct((share, got.shape[0] * width), F32)
    return pl.pallas_call(
        functools.partial(unpack_kernel, width),
        out_shape=[shape, shape],
        in_specs=[pl.BlockSpec(memory_space=pltpu.VMEM)],
        out_specs=[pl.BlockSpec(memory_space=pltpu.VMEM)] * 2,
        cost_estimate=pl.CostEstimate(flops=10**6, bytes_accessed=2**20, transcendentals=0),
    )(got)


def per_device(nf, nt, grad, start_basis, weight, first_moment, second_moment):
    inv_sqrt = 1.0 / math.sqrt(M)
    share_rows, cols = first_moment.shape
    share_cols = cols // nf
    rank = start_basis.shape[1]

    sent = jnp.concatenate([first_moment.astype(BF), second_moment.astype(BF)], axis=0)
    sent = sent.reshape(2 * share_rows, nf, share_cols).transpose(1, 0, 2)
    sent = row_major(jnp.pad(sent, ((0, 0), (0, 0), (0, -share_cols % 128))))

    first_row = (lax.axis_index("fsdp") * (rank // nf)).astype(jnp.uint32)
    panel, first_row = lax.optimization_barrier((mm(grad, start_basis, 0, 0).astype(BF), first_row))
    panel = (scatter_sum(panel, "fsdp", nf) * inv_sqrt).astype(BF)
    panel = gather(panel, "fsdp", nf)
    image = scatter_sum(mm(grad, panel, 1, 0), "tp", nt).astype(BF)
    image = lax.all_gather(image, "tp", axis=0, tiled=True)
    raw = scatter_sum(row_major(mm(grad, image, 0, 0).astype(BF)), "fsdp", nf).astype(BF)

    raw = gather(raw, "fsdp", nf)
    rows = rank // nt
    few = rank // nf // nt
    mine = lax.dynamic_slice(mm(panel, raw, 0, 0), (first_row, jnp.uint32(0)), (rank // nf, rank))
    mine = jnp.pad(mine.astype(BF).reshape(nt, few, rank), ((0, 0), (0, -few % 8), (0, 0)))
    both = jnp.concatenate([mm(grad, raw, 1, 0).astype(BF).reshape(nt, rows, rank), mine], axis=1)
    both = jnp.sum(lax.all_to_all(both, "tp", 0, 0, tiled=True).astype(F32), axis=0).astype(BF)
    both = lax.all_gather(both, "tp", axis=0, tiled=False)
    wide = both[:, :rows].reshape(-1, rank)
    gram = both[:, rows : rows + few].reshape(1, rank // nf, rank)
    outer = (mm(wide, wide, 0, 0) / M).astype(BF).reshape(nf, -1, rank)
    raw = row_major(mm(grad, wide, 0, 0).astype(BF))
    got = jnp.concatenate([sent, tiles(outer)], axis=1)
    got = lax.all_to_all(got, "fsdp", 0, 0, tiled=True)
    first_old = got[:, :share_rows].reshape(rank, -1)
    second_old = got[:, share_rows : 2 * share_rows].reshape(rank, -1)
    sums = jnp.sum(got[:, 2 * share_rows :].astype(F32), axis=0).astype(BF)
    grams = gather(jnp.concatenate([sums, tiles(gram)[0]], axis=0), "fsdp", nf)
    grams, raw = lax.optimization_barrier((grams, raw))
    grams = grams.reshape(nf, 2, -1, rank // 128, 8, 128).transpose(1, 0, 2, 4, 3, 5).reshape(2, rank, rank)
    outer, gram = grams[0].astype(F32), grams[1].astype(F32) / M
    inverse = chol_inv(gram)
    second = chol_inv(mm_high(mm_high(inverse, outer, 1, 0), inverse, 1, 1) / M)
    both = mm_high(second, inverse, 1, 0)
    margin = mm_high(gram, both, 0, 1)
    first_basis = mm_split(image, inverse, 1, 1).astype(BF)
    new_basis = (mm_split(wide, both, 1, 1) * inv_sqrt).astype(BF)
    rotated_one = mm(first_old, margin.astype(BF), 0, 0)[:share_cols]
    rotated_two = mm(second_old, (margin * margin).astype(BF), 0, 0)[:share_cols]
    parts = lax.all_to_all(raw.reshape(nf, share_cols, rank), "fsdp", 0, 0, tiled=True)
    rotated_one, rotated_two, first_basis, new_basis = lax.optimization_barrier(
        (rotated_one, rotated_two, first_basis, new_basis)
    )
    got = finish(1.0 / M, parts, *halves(both), rotated_one, rotated_two)
    got = lax.all_to_all(got, "fsdp", 0, 0, tiled=True)
    direction = got[:, 16:].reshape(cols, rank)
    moment_one, moment_two = unpack(got, share_cols, share_rows)
    expanded = mm(new_basis, direction, 1, 1)
    new_weight = (weight.astype(F32) - STEP_SIZE * inv_sqrt * expanded).astype(BF)
    return (first_basis, new_basis, moment_one, moment_two, new_weight)


def solution(mesh):
    specs = (P("fsdp", "tp"), P("fsdp", None), P("fsdp", "tp"), P("fsdp", "tp"), P("fsdp", "tp"))
    out_specs = (P("fsdp", None), P("fsdp", None), P("fsdp", "tp"), P("fsdp", "tp"), P("fsdp", "tp"))
    nf, nt = mesh.shape["fsdp"], mesh.shape["tp"]

    def body(*args):
        return per_device(nf, nt, *args)

    return jax.shard_map(body, mesh=mesh, in_specs=specs, out_specs=out_specs, check_vma=False)
```

```python
import functools
import math

import jax
import jax.numpy as jnp
from jax import lax
from jax.experimental import pallas as pl
from jax.experimental.pallas import tpu as pltpu
from jax.experimental.layout import Layout, with_layout_constraint
from jax.sharding import PartitionSpec as P

M = 8192

BETA_ONE = 0.9
BETA_TWO = 0.95
ADAM_EPS = 1e-06
STEP_SIZE = 2.0

BF = jnp.bfloat16
F32 = jnp.float32

def elim(read, n=128):
    lane = lax.broadcasted_iota(jnp.int32, (8, n), 1)
    sub = lax.broadcasted_iota(jnp.int32, (8, n), 0)
    G = [read(g) for g in range(n // 8)]
    out = []
    for g0 in range(n // 8):
        acc = jnp.zeros((8, n), jnp.float32)
        for s0 in range(8):
            j = g0 * 8 + s0
            hit = lane == j
            r = jnp.broadcast_to(G[g0][s0:s0 + 1, :], (8, n))
            p = jnp.broadcast_to(r[:, j:j + 1], (8, n))
            row = jnp.where(lane < j, r, jnp.where(hit, 1.0, 0.0)) * lax.rsqrt(p)
            acc = jnp.where(sub == s0, row, acc)
            rr = jnp.where(hit, 1.0, r) * (1.0 / p)
            for g in range(g0, n // 8):
                c = jnp.broadcast_to(G[g][:, j:j + 1], (8, n))
                new = jnp.where(hit, 0.0, G[g]) - c * rr
                G[g] = jnp.where(sub > s0, new, G[g]) if g == g0 else new
        out.append(acc)
    return out


NB = 128


def exact_dot(a, b, dims):
    return lax.dot_general(a, b, (dims, ((), ())), precision=lax.Precision.HIGHEST, preferred_element_type=F32)


def fast_dot(a, b, dims):
    return lax.dot_general(a, b, (dims, ((), ())), preferred_element_type=F32)


def halves(x):
    hi = x.astype(BF)
    return hi, (x - hi.astype(F32)).astype(BF)


def eliminate(a_ref, x_ref, w_ref, s_ref, b_ref):
    n = a_ref.shape[0]
    nb = n // NB
    s_ref[...] = a_ref[...]
    b_ref[...] = jnp.zeros_like(b_ref)
    x_ref[...] = jnp.zeros_like(x_ref)

    @pl.loop(0, nb)
    def _(k):
        rows = pl.ds(pl.multiple_of(k * NB, NB), NB)
        for g, v in enumerate(elim(lambda g: s_ref[pl.ds(pl.multiple_of(k * NB + 8 * g, 8), 8), rows])):
            w_ref[pl.ds(8 * g, 8), :] = v
        w = w_ref[...]
        u = exact_dot(w, s_ref[rows, :], ((1,), (0,)))
        x_ref[rows, :] = exact_dot(w, b_ref[rows, :], ((1,), (0,)))
        x_ref[rows, rows] = w

        @pl.loop(k + 1, nb)
        def _(i):
            below = pl.ds(pl.multiple_of(i * NB, NB), NB)
            ui = exact_dot(w, s_ref[rows, below], ((1,), (0,)))
            s_ref[below, :] -= exact_dot(ui, u, ((0,), (0,)))
            b_ref[below, :] -= exact_dot(ui, x_ref[rows, :], ((0,), (0,)))


def chol_kernel(a_ref, x_ref, w_ref, s_ref, b_ref, ah_ref, al_ref, yh_ref, yl_ref, e_ref, d_ref):
    n = a_ref.shape[0]
    nb = n // NB
    eye = (lax.broadcasted_iota(jnp.int32, (NB, NB), 0) == lax.broadcasted_iota(jnp.int32, (NB, NB), 1)).astype(F32)
    lower = (lax.broadcasted_iota(jnp.int32, (NB, NB), 0) > lax.broadcasted_iota(jnp.int32, (NB, NB), 1)).astype(F32) + 0.5 * eye

    for r in range(nb):
        at = pl.ds(r * NB, NB)
        d_ref[:, at] = lax.rsqrt(jnp.sum(a_ref[at, at] * eye, axis=0, keepdims=True))
    for r in range(nb):
        at = pl.ds(r * NB, NB)
        here = jnp.sum(eye * d_ref[:, at], axis=1, keepdims=True)
        hi, lo = halves(a_ref[at, :] * here * d_ref[...])
        ah_ref[at, :] = hi
        al_ref[at, :] = lo
    x_ref[...] = jnp.zeros_like(x_ref)
    yh_ref[...] = jnp.zeros_like(yh_ref)
    yl_ref[...] = jnp.zeros_like(yl_ref)
    for r in range(nb):
        at = pl.ds(r * NB, NB)
        end = (r + 1) * NB
        a = ah_ref[at, :end].astype(F32)
        if r:
            x_ref[at, : r * NB] = -a[:, : r * NB]
        x_ref[at, at] = eye - (a[:, r * NB :] - eye) * lower

    def step(fine):
        for r in range(nb):
            at, end = pl.ds(r * NB, NB), (r + 1) * NB
            hi, lo = halves(x_ref[at, :end])
            yh_ref[at, :end] = hi
            if fine:
                yl_ref[at, :end] = lo
        total = jnp.zeros((1, 1), F32)
        for r in range(nb):
            at, start, end = pl.ds(r * NB, NB), r * NB, (r + 1) * NB
            yh = yh_ref[at, :end]
            t = fast_dot(yh, ah_ref[:end, :end], ((1,), (0,)))
            if fine:
                t += fast_dot(yh, al_ref[:end, :end], ((1,), (0,))) + fast_dot(yl_ref[at, :end], ah_ref[:end, :end], ((1,), (0,)))
            hi, lo = halves(t)
            e = fast_dot(hi, yh_ref[:end, :end], ((1,), (1,)))
            if fine:
                e += fast_dot(lo, yh_ref[:end, :end], ((1,), (1,))) + fast_dot(hi, yl_ref[:end, :end], ((1,), (1,)))
            corner = (e[:, start:] - eye) * lower
            total += jnp.sum(corner * corner, keepdims=True)
            e_ref[at, start:end] = corner.astype(BF)
            if r:
                left = e[:, :start]
                total += jnp.sum(left * left, keepdims=True)
                e_ref[at, :start] = left.astype(BF)
        for r in reversed(range(nb)):
            at, end = pl.ds(r * NB, NB), (r + 1) * NB
            x_ref[at, :end] -= fast_dot(e_ref[at, :end], yh_ref[:end, :end], ((1,), (0,)))
        return total[0, 0]

    def more(tol, most):
        return lambda state: jnp.logical_and(state[0] < most, state[1] > tol)

    _, size = lax.while_loop(more(0.05, 10), lambda s: (s[0] + 1, step(False)), (0, jnp.float32(1e9)))
    _, size = lax.while_loop(more(1e-5, 6), lambda s: (s[0] + 1, step(True)), (0, jnp.float32(1e9)))
    good = size <= 1e-5

    @pl.when(good)
    def _():
        for r in range(nb):
            at, end = pl.ds(r * NB, NB), (r + 1) * NB
            x_ref[at, :end] *= d_ref[:, :end]

    @pl.when(jnp.logical_not(good))
    def _():
        eliminate(a_ref, x_ref, w_ref, s_ref, b_ref)


def chol_inv(a):
    n = a.shape[0]
    square = lambda kind: pltpu.VMEM((n, n), kind)
    return pl.pallas_call(
        chol_kernel,
        out_shape=jax.ShapeDtypeStruct((n, n), F32),
        in_specs=[pl.BlockSpec(memory_space=pltpu.VMEM)],
        out_specs=pl.BlockSpec(memory_space=pltpu.VMEM),
        scratch_shapes=[pltpu.VMEM((NB, NB), F32), square(F32), square(F32), square(BF), square(BF), square(BF), square(BF), square(BF), pltpu.VMEM((1, n), F32)],
        cost_estimate=pl.CostEstimate(flops=10**6, bytes_accessed=2**10, transcendentals=0),
        compiler_params=pltpu.CompilerParams(vmem_limit_bytes=32 * 2**20),
    )(a)


def mm(a, b, ca, cb):
    return lax.dot_general(a, b, (((ca,), (cb,)), ((), ())), preferred_element_type=F32)


def mm_split(a, b, ca, cb):
    hi = b.astype(BF)
    lo = (b - hi.astype(F32)).astype(BF)
    return mm(a, hi, ca, cb) + mm(a, lo, ca, cb)


def mm_high(a, b, ca, cb):
    return lax.dot_general(a, b, (((ca,), (cb,)), ((), ())), precision=lax.Precision.HIGH, preferred_element_type=F32)


def scatter_sum(x, axis, n):
    parts = lax.all_to_all(x.astype(BF).reshape(n, x.shape[0] // n, x.shape[1]), axis, 0, 0, tiled=True)
    return jnp.sum(parts.astype(F32), axis=0)


def gather(x, axis, n):
    parts = lax.all_to_all(jnp.broadcast_to(x[None], (n,) + x.shape), axis, 0, 0, tiled=True)
    return parts.reshape(n * x.shape[0], x.shape[1])


def row_major(x):
    return with_layout_constraint(x, Layout(tuple(range(x.ndim))))


def tiles(x):
    n, rows, cols = x.shape
    return x.reshape(n, rows // 8, 8, cols // 128, 128).transpose(0, 1, 3, 2, 4).reshape(n, -1, 128)


def finish_kernel(scale, parts_ref, high_ref, low_ref, one_ref, two_ref, out_ref):
    nf, rows, rank = parts_ref.shape
    share = rank // nf
    raw = parts_ref[0].astype(F32)
    for g in range(1, nf):
        raw += parts_ref[g].astype(F32)
    hi, lo = halves(raw)
    dims = ((1,), (1,))
    reduced = (fast_dot(hi, high_ref[...], dims) + fast_dot(lo, high_ref[...], dims) + fast_dot(hi, low_ref[...], dims)) * scale
    one = BETA_ONE * one_ref[...] + (1.0 - BETA_ONE) * reduced
    two = BETA_TWO * two_ref[...] + (1.0 - BETA_TWO) * reduced * reduced
    direction = (one / (jnp.sqrt(two) + ADAM_EPS)).astype(BF)
    pad = jnp.zeros((-rows % 128, rank), F32)
    one = jnp.concatenate([one, pad], axis=0).T
    two = jnp.concatenate([two, pad], axis=0).T
    both = [one.astype(BF), two.astype(BF)]
    for g in range(nf):
        out_ref[g, 16:, :] = direction
        for i in range(2 * share // 16):
            first = g * share + i * 16 % share
            out_ref[g, :16, i * 128 : (i + 1) * 128] = both[i * 16 // share][first : first + 16]


def finish(scale, parts, high, low, one, two):
    nf, rows, rank = parts.shape
    return pl.pallas_call(
        functools.partial(finish_kernel, scale),
        out_shape=jax.ShapeDtypeStruct((nf, 16 + rows, rank), BF),
        in_specs=[pl.BlockSpec(memory_space=pltpu.VMEM)] * 5,
        out_specs=pl.BlockSpec(memory_space=pltpu.VMEM),
        cost_estimate=pl.CostEstimate(flops=10**9, bytes_accessed=6 * 2**20, transcendentals=0),
        compiler_params=pltpu.CompilerParams(vmem_limit_bytes=32 * 2**20),
    )(parts, high, low, one, two)


def unpack_kernel(width, got_ref, one_ref, two_ref):
    share = one_ref.shape[0]
    for ref, first in ((one_ref, 0), (two_ref, share)):
        for i in range(share // 16):
            lanes = slice((first // 16 + i) * 128, (first // 16 + i) * 128 + width)
            rows = [got_ref[g, :16, :].astype(F32)[:, lanes] for g in range(got_ref.shape[0])]
            ref[i * 16 : (i + 1) * 16, :] = jnp.concatenate(rows, axis=1)


def unpack(got, width, share):
    shape = jax.ShapeDtypeStruct((share, got.shape[0] * width), F32)
    return pl.pallas_call(
        functools.partial(unpack_kernel, width),
        out_shape=[shape, shape],
        grid=(1,),
        in_specs=[pl.BlockSpec((got.shape[0], 16, got.shape[2]), lambda i: (0, 0, 0))],
        out_specs=[pl.BlockSpec(shape.shape, lambda i: (0, 0))] * 2,
        cost_estimate=pl.CostEstimate(flops=10**6, bytes_accessed=2**20, transcendentals=0),
    )(got)


def per_device(nf, nt, grad, start_basis, weight, first_moment, second_moment):
    inv_sqrt = 1.0 / math.sqrt(M)
    share_rows, cols = first_moment.shape
    share_cols = cols // nf
    rank = start_basis.shape[1]

    sent = jnp.concatenate([first_moment.astype(BF), second_moment.astype(BF)], axis=0)
    sent = sent.reshape(2 * share_rows, nf, share_cols).transpose(1, 0, 2)
    sent = row_major(jnp.pad(sent, ((0, 0), (0, 0), (0, -share_cols % 128))))

    first_row = (lax.axis_index("fsdp") * (rank // nf)).astype(jnp.uint32)
    panel, first_row = lax.optimization_barrier((mm(grad, start_basis, 0, 0).astype(BF), first_row))
    panel = (scatter_sum(panel, "fsdp", nf) * inv_sqrt).astype(BF)
    panel = gather(panel, "fsdp", nf)
    image = scatter_sum(mm(grad, panel, 1, 0), "tp", nt).astype(BF)
    image = lax.all_gather(image, "tp", axis=0, tiled=True)
    raw = scatter_sum(row_major(mm(grad, image, 0, 0).astype(BF)), "fsdp", nf).astype(BF)

    raw = gather(raw, "fsdp", nf)
    rows = rank // nt
    few = rank // nf // nt
    mine = lax.dynamic_slice(mm(panel, raw, 0, 0), (first_row, jnp.uint32(0)), (rank // nf, rank))
    mine = jnp.pad(mine.astype(BF).reshape(nt, few, rank), ((0, 0), (0, -few % 8), (0, 0)))
    both = jnp.concatenate([mm(grad, raw, 1, 0).astype(BF).reshape(nt, rows, rank), mine], axis=1)
    both = jnp.sum(lax.all_to_all(both, "tp", 0, 0, tiled=True).astype(F32), axis=0).astype(BF)
    both = lax.all_gather(both, "tp", axis=0, tiled=False)
    wide = both[:, :rows].reshape(-1, rank)
    gram = both[:, rows : rows + few].reshape(1, rank // nf, rank)
    outer = (mm(wide, wide, 0, 0) / M).astype(BF).reshape(nf, -1, rank)
    raw = row_major(mm(grad, wide, 0, 0).astype(BF))
    got = jnp.concatenate([sent, tiles(outer)], axis=1)
    got = lax.all_to_all(got, "fsdp", 0, 0, tiled=True)
    first_old = got[:, :share_rows].reshape(rank, -1)
    second_old = got[:, share_rows : 2 * share_rows].reshape(rank, -1)
    sums = jnp.sum(got[:, 2 * share_rows :].astype(F32), axis=0).astype(BF)
    grams = gather(jnp.concatenate([sums, tiles(gram)[0]], axis=0), "fsdp", nf)
    grams, raw = lax.optimization_barrier((grams, raw))
    grams = grams.reshape(nf, 2, -1, rank // 128, 8, 128).transpose(1, 0, 2, 4, 3, 5).reshape(2, rank, rank)
    outer, gram = grams[0].astype(F32), grams[1].astype(F32) / M
    inverse = chol_inv(gram)
    second = chol_inv(mm_high(mm_high(inverse, outer, 1, 0), inverse, 1, 1) / M)
    both = mm_high(second, inverse, 1, 0)
    margin = mm_split((gram * M).astype(BF), both, 0, 1) / M
    first_basis = mm_split(image, inverse, 1, 1).astype(BF)
    new_basis = (mm_split(wide, both, 1, 1) * inv_sqrt).astype(BF)
    rotated_one = mm(first_old, margin.astype(BF), 0, 0)[:share_cols]
    rotated_two = mm(second_old, (margin * margin).astype(BF), 0, 0)[:share_cols]
    parts = lax.all_to_all(raw.reshape(nf, share_cols, rank), "fsdp", 0, 0, tiled=True)
    rotated_one, rotated_two, first_basis, new_basis = lax.optimization_barrier(
        (rotated_one, rotated_two, first_basis, new_basis)
    )
    got = finish(1.0 / M, parts, *halves(both), rotated_one, rotated_two)
    got = lax.all_to_all(got, "fsdp", 0, 0, tiled=True)
    direction = got[:, 16:].reshape(cols, rank)
    moment_one, moment_two = unpack(got, share_cols, share_rows)
    expanded = mm(new_basis, direction, 1, 1)
    new_weight = (weight.astype(F32) - STEP_SIZE * inv_sqrt * expanded).astype(BF)
    return (first_basis, new_basis, moment_one, moment_two, new_weight)


def solution(mesh):
    specs = (P("fsdp", "tp"), P("fsdp", None), P("fsdp", "tp"), P("fsdp", "tp"), P("fsdp", "tp"))
    out_specs = (P("fsdp", None), P("fsdp", None), P("fsdp", "tp"), P("fsdp", "tp"), P("fsdp", "tp"))
    nf, nt = mesh.shape["fsdp"], mesh.shape["tp"]

    def body(*args):
        return per_device(nf, nt, *args)

    return jax.shard_map(body, mesh=mesh, in_specs=specs, out_specs=out_specs, check_vma=False)
```
